512 devices in a mesh: dp: 8 (over z_lo, core), ctx: 64 (over z_hi, y, x).
Axes of the slice: x: 4, y: 8, z: 8 (z_hi: 2, z_lo: 4; z = z_hi * 4 + z_lo), core: 2. Of those that a mesh axis runs over, the one named last changes fastest.
Arguments:
- query_gate: bfloat16 [8, 512, 8192], P('dp', None, 'ctx'), may hold values from -6 to 6
- key_gate: bfloat16 [8, 512, 8192], P('dp', None, 'ctx'), may hold values from -6 to 6
- value_gate: bfloat16 [8, 512, 8192], P('dp', None, 'ctx'), may hold values from -6 to 6
- grad_out: bfloat16 [8, 512, 8192], P('dp', None, 'ctx'), may hold values from -6 to 6
- long_filter: float32 [512, 8192], P('ctx'), may hold values from -1 to 1
Outputs:
- grad_query: bfloat16 [8, 512, 8192], P('dp', None, 'ctx')
- grad_key: bfloat16 [8, 512, 8192], P('dp', None, 'ctx')
- grad_value: bfloat16 [8, 512, 8192], P('dp', None, 'ctx')
- grad_filter: float32 [512, 8192], P('ctx', 'dp')
The draws below stay inside these ranges and needn't reach their ends.
All inputs are finite; a program needn't handle non-finite values.
Results may differ from the reference program's by a relative error of at most 0.017.
Values may be sent and summed in bfloat16 or wider, within the bound.
No kernel may reach another device: no remote copies, remote signals or barrier semaphores. Data moves between devices by JAX's collectives and lax.ppermute only.
A program may use at most 64 MiB of HBM per device.

```python
import math
import jax
import jax.numpy as jnp
from jax import lax

C = 512
SEQ = 8192
SEQS = 8


def draw_long_filter(key, part):
    key = jax.random.fold_in(key, 11)
    rate_key, noise_key = jax.random.split(key)
    lags = jnp.arange(SEQ).astype(jnp.float32)
    low = jnp.log(0.5 / SEQ)
    high = jnp.log(1.0 / 30.0)
    noise = jax.random.truncated_normal(noise_key, -4.0, 4.0, (C, SEQ), jnp.float32)
    rate = jnp.exp(jax.random.uniform(rate_key, (C, 1), jnp.float32, low, high))
    scale = jnp.sqrt((1.0 - jnp.exp(-2.0 * rate)) / (1.0 - jnp.exp(-2.0 * rate * SEQ)))
    return (noise * scale * jnp.exp(-rate * lags)).astype(jnp.float32)


def steps_of(rng, dims, cuts, low, largest):
    def one(position, blocks):
        draws = jax.random.uniform(jax.random.fold_in(jax.random.fold_in(rng, 6), position), (blocks,), jnp.float32, low / len(cuts), largest / len(cuts))
        return jnp.repeat(jnp.exp(draws), dims[position] // blocks).reshape((-1,) + (1,) * (len(dims) - position - 1))

    factor_of = one(*cuts[0])
    for cut in cuts[1:]:
        factor_of = factor_of * one(*cut)
    return factor_of


def normal_values(rng, dims, spread, limit, shards=(), held_as=jnp.bfloat16):
    array = jax.random.normal(rng, dims, jnp.float32) * spread
    if len(shards) > 0:
        array = steps_of(rng, dims, shards, -0.22, 0.18) * array
    return jnp.clip(array, min=-limit, max=limit).astype(held_as)


def setup_inputs(seed: int = 0) -> dict:
    keys = jax.random.split(jax.random.key(seed), 6)
    query_gate = normal_values(keys[0], (SEQS, C, SEQ), 1.0, 6.0, ((0, 8), (2, 64)))
    key_gate = normal_values(keys[1], (SEQS, C, SEQ), 1.0, 6.0, ((0, 8), (2, 64)))
    value_gate = normal_values(keys[2], (SEQS, C, SEQ), 1.0, 6.0, ((0, 8), (2, 64)))
    grad_out = normal_values(keys[3], (SEQS, C, SEQ), 1.0, 6.0, ((0, 8), (2, 64)))
    long_filter = draw_long_filter(jax.random.fold_in(keys[5], 71), 0)
    return {"query_gate": query_gate, "key_gate": key_gate, "value_gate": value_gate, "grad_out": grad_out, "long_filter": long_filter}


def reference(query_gate, key_gate, value_gate, grad_out, long_filter):
    length = 2 * SEQ
    filter_spec = jnp.fft.rfft(long_filter, n=length, axis=-1)

    def one_sequence(total, items):
        query, keys_in, values_in, cotangent = items
        kv = lax.optimization_barrier((keys_in.astype(jnp.float32) * values_in.astype(jnp.float32)).astype(jnp.bfloat16))
        dz = lax.optimization_barrier((cotangent.astype(jnp.float32) * query.astype(jnp.float32)).astype(jnp.bfloat16))
        kv_spec = jnp.fft.rfft(kv.astype(jnp.float32), n=length, axis=-1)
        dz_spec = jnp.fft.rfft(dz.astype(jnp.float32), n=length, axis=-1)
        conv = jnp.fft.irfft(filter_spec * kv_spec, n=length, axis=-1)[:, :SEQ]
        conv = lax.optimization_barrier(conv.astype(jnp.bfloat16))
        dkv = jnp.fft.irfft(jnp.conj(filter_spec) * dz_spec, n=length, axis=-1)[:, :SEQ]
        dkv = lax.optimization_barrier(dkv.astype(jnp.bfloat16))
        total = total + jnp.fft.irfft(jnp.conj(kv_spec) * dz_spec, n=length, axis=-1)[:, :SEQ]
        grad_q = (cotangent.astype(jnp.float32) * conv.astype(jnp.float32)).astype(jnp.bfloat16)
        grad_k = (dkv.astype(jnp.float32) * values_in.astype(jnp.float32)).astype(jnp.bfloat16)
        grad_v = (dkv.astype(jnp.float32) * keys_in.astype(jnp.float32)).astype(jnp.bfloat16)
        return (total, (grad_q, grad_k, grad_v))
    start = jnp.zeros((C, SEQ), jnp.float32)
    total, outputs = lax.scan(one_sequence, start, (query_gate, key_gate, value_gate, grad_out))
    grad_filter = total / math.sqrt(SEQ * SEQS)
    return (outputs[0], outputs[1], outputs[2], grad_filter)
```

```python
import math

import jax
import jax.numpy as jnp
import numpy as np
from jax import lax
from jax.experimental import pallas as pl
from jax.experimental.pallas import tpu as pltpu
from jax.sharding import PartitionSpec as P

BLOCK = 128
bf16 = jnp.bfloat16
f32 = jnp.float32


def split_table(table):
    high = table.astype(bf16)
    return high, (table - high.astype(np.float64)).astype(bf16)


def make_tables(half, seq):
    length = 2 * seq
    k = np.arange(half) + 0.5
    first = 2.0 * math.pi * np.outer(k, np.arange(half)) / (2 * half)
    turn = 2.0 * math.pi * np.outer(k, np.arange(BLOCK)) / length
    block = 2.0 * math.pi * np.outer(np.arange(BLOCK), np.arange(BLOCK)) / BLOCK
    first_high, first_low = split_table(np.concatenate([np.cos(first), -np.sin(first)], 0))
    last_high, last_low = split_table(
        np.concatenate([np.cos(first).T, -np.sin(first).T], 1) * (2.0 / length)
    )
    cos, sin = np.cos(block), np.sin(block)
    mid_high, mid_low = split_table(np.block([[cos, -sin], [sin, cos]]))
    return {
        "forward": np.concatenate([first_high, first_high, first_low], 1),
        "back": np.concatenate([last_high, last_high, last_low], 1),
        "middle": np.concatenate([mid_high, mid_high, mid_low], 0),
        "turn": np.stack([np.cos(turn), np.sin(turn)]).astype(np.float32),
    }


def split(value):
    high = value.astype(bf16)
    return high, (value - high.astype(f32)).astype(bf16)


def dot(left, right):
    return jnp.dot(left, right, preferred_element_type=f32)


def middle_transform(rows, middle_ref):
    high, low = split(rows)
    return dot(jnp.concatenate([high, low, high], 1), middle_ref[...])


def forward_rows(rows_ref, chans, half, exact, forward_ref, turn_ref, middle_ref):
    cols = jnp.concatenate([rows_ref[pl.ds(c, half, stride=chans), :] for c in range(chans)], 1)
    if exact:
        high = cols.astype(bf16)
        table = jnp.concatenate([forward_ref[:, :half], forward_ref[:, 2 * half :]], 1)
        section = dot(table, jnp.concatenate([high, high], 0))
    else:
        high, low = split(cols)
        section = dot(forward_ref[...], jnp.concatenate([high, low, high], 0))
    cos, sin = turn_ref[0], turn_ref[1]
    rows = []
    for c in range(chans):
        re = section[:half, c * BLOCK : (c + 1) * BLOCK]
        im = section[half:, c * BLOCK : (c + 1) * BLOCK]
        rows.append(jnp.concatenate([re * cos + im * sin, im * cos - re * sin], 1))
    return middle_transform(jnp.concatenate(rows, 0), middle_ref)


def inverse_rows(spec, chans, half, out_ref, back_ref, turn_ref, middle_ref):
    inner = middle_transform(spec, middle_ref)
    cos, sin = turn_ref[0], turn_ref[1]
    cols = []
    for c in range(chans):
        re = inner[c * half : (c + 1) * half, :BLOCK]
        minus = inner[c * half : (c + 1) * half, BLOCK:]
        cols.append(jnp.concatenate([re * cos + minus * sin, re * sin - minus * cos], 0))
    high, low = split(jnp.concatenate(cols, 1))
    signal = dot(back_ref[...], jnp.concatenate([high, low, high], 0))
    for c in range(chans):
        out_ref[pl.ds(c, half, stride=chans), :] = signal[:, c * BLOCK : (c + 1) * BLOCK]


def gate_kernel(key_ref, value_ref, grad_ref, query_ref, out_ref):
    groups, both, _ = out_ref.shape
    shape = (groups, both // 2, BLOCK)
    kv = key_ref[...].astype(f32) * value_ref[...].astype(f32)
    dz = grad_ref[...].astype(f32) * query_ref[...].astype(f32)
    out_ref[...] = jnp.concatenate([kv.reshape(shape), dz.reshape(shape)], 1).astype(bf16)


def filter_kernel(filter_ref, forward_ref, turn_ref, middle_ref, spec_ref, rows):
    chans, seq = filter_ref.shape
    half = seq // BLOCK
    for a in range(half):
        rows[pl.ds(a * chans, chans), :] = filter_ref[:, a * BLOCK : (a + 1) * BLOCK]
    spec_ref[...] = forward_rows(rows, chans, half, False, forward_ref, turn_ref, middle_ref)


def forward_kernel(
    both_ref, forward_ref, back_ref, turn_ref, middle_ref, spec_ref, lag_ref, rows, out_rows
):
    half, both, _ = both_ref.shape
    chans = both // 2
    rows[...] = both_ref[...].astype(f32).reshape(half * both, BLOCK)
    spec = forward_rows(rows, both, half, True, forward_ref, turn_ref, middle_ref)
    spec_ref[...] = spec
    count = chans * half
    kv_re, kv_im = spec[:count, :BLOCK], spec[:count, BLOCK:]
    dz_re, dz_im = spec[count:, :BLOCK], spec[count:, BLOCK:]
    cross = jnp.concatenate([kv_re * dz_re + kv_im * dz_im, kv_im * dz_re - kv_re * dz_im], 1)
    inverse_rows(cross, chans, half, out_rows, back_ref, turn_ref, middle_ref)
    lag_ref[...] = out_rows[...].reshape(half, chans, BLOCK).astype(bf16)


def conv_kernel(spec_ref, filter_ref, back_ref, turn_ref, middle_ref, out_ref, out_rows):
    half, both, _ = out_ref.shape
    count = half * both // 2
    f_re, f_im = filter_ref[:, :BLOCK], filter_ref[:, BLOCK:]
    kv_re, kv_im = spec_ref[:count, :BLOCK], spec_ref[:count, BLOCK:]
    dz_re, dz_im = spec_ref[count:, :BLOCK], spec_ref[count:, BLOCK:]
    conv = jnp.concatenate([f_re * kv_re - f_im * kv_im, -f_re * kv_im - f_im * kv_re], 1)
    dkv = jnp.concatenate([f_re * dz_re + f_im * dz_im, f_im * dz_re - f_re * dz_im], 1)
    inverse_rows(
        jnp.concatenate([conv, dkv], 0), both, half, out_rows, back_ref, turn_ref, middle_ref
    )
    out_ref[...] = out_rows[...].reshape(half, both, BLOCK).astype(bf16)


def final_kernel(both_ref, key_ref, value_ref, grad_ref, gq_ref, gk_ref, gv_ref):
    groups, both, _ = both_ref.shape
    chans = both // 2
    wide = both_ref[...].astype(f32)
    conv = wide[:, :chans, :].reshape(groups * chans, BLOCK)
    dkv = wide[:, chans:, :].reshape(groups * chans, BLOCK)
    gq_ref[...] = (grad_ref[...].astype(f32) * conv).astype(bf16)
    gk_ref[...] = (dkv * value_ref[...].astype(f32)).astype(bf16)
    gv_ref[...] = (dkv * key_ref[...].astype(f32)).astype(bf16)


def lag_kernel(terms_ref, out_ref, *, scale):
    wide = terms_ref[...].astype(f32)
    total = wide[0]
    for g in range(1, wide.shape[0]):
        total = total + wide[g]
    total = total * scale
    for a in range(total.shape[0]):
        out_ref[:, a * BLOCK : (a + 1) * BLOCK] = total[a]


def call(kernel, out, *args, scratch=(), flops=0, name=None):
    nbytes = sum(math.prod(a.shape) * a.dtype.itemsize for a in args)
    vmem = pl.BlockSpec(memory_space=pltpu.VMEM)
    return pl.pallas_call(
        kernel,
        out_shape=out,
        in_specs=[vmem] * len(args),
        out_specs=jax.tree.map(lambda _: vmem, out),
        scratch_shapes=[pltpu.VMEM(shape, f32) for shape in scratch],
        compiler_params=pltpu.CompilerParams(vmem_limit_bytes=40 * 2**20),
        cost_estimate=pl.CostEstimate(flops=flops, bytes_accessed=nbytes, transcendentals=0),
        name=name,
    )(*args)


def local(query_gate, key_gate, value_gate, grad_out, long_filter):
    chans, seq = long_filter.shape
    half = seq // BLOCK
    groups = lax.axis_size("dp")
    total = query_gate.shape[1]
    both = 2 * chans
    tables = {name: jnp.asarray(table) for name, table in make_tables(half, seq).items()}
    forward, back = tables["forward"], tables["back"]
    turn, middle = tables["turn"], tables["middle"]
    query, key, value, grad = (
        x.reshape(total, BLOCK) for x in (query_gate, key_gate, value_gate, grad_out)
    )
    shape = jax.ShapeDtypeStruct
    pieces = shape((half, both, BLOCK), bf16)
    work = 2 * chans * half * 256 * 768

    gated = call(gate_kernel, pieces, key, value, grad, query, name="gate")
    here = lax.all_to_all(gated, "ctx", 0, 0, tiled=True)
    filter_spec = call(
        filter_kernel,
        shape((chans * half, 2 * BLOCK), f32),
        long_filter,
        forward,
        turn,
        middle,
        scratch=[(half * chans, BLOCK)],
        flops=2 * work,
        name="filter",
    )
    spec, lag = call(
        forward_kernel,
        (shape((both * half, 2 * BLOCK), f32), shape((half, chans, BLOCK), bf16)),
        here,
        forward,
        back,
        turn,
        middle,
        scratch=[(half * both, BLOCK), (half * chans, BLOCK)],
        flops=4 * work,
        name="forward",
    )
    terms = lax.all_to_all(lag, "dp", 0, 0, tiled=True)
    carried = call(
        conv_kernel,
        pieces,
        spec,
        filter_spec,
        back,
        turn,
        middle,
        scratch=[(half * both, BLOCK)],
        flops=4 * work,
        name="conv",
    )
    back_here = lax.all_to_all(carried, "ctx", 0, 0, tiled=True)
    own = half // groups
    grad_filter = call(
        lambda *refs: lag_kernel(*refs, scale=1.0 / math.sqrt(seq * groups)),
        shape((chans, own * BLOCK), f32),
        terms.reshape(groups, own, chans, BLOCK),
        name="lag_sum",
    )
    grads = call(
        final_kernel,
        (shape((total, BLOCK), bf16),) * 3,
        back_here,
        key,
        value,
        grad,
        name="final",
    )
    return tuple(g[None] for g in grads) + (grad_filter,)


def solution(mesh):
    in_specs = (
        P("dp", None, "ctx"),
        P("dp", None, "ctx"),
        P("dp", None, "ctx"),
        P("dp", None, "ctx"),
        P("ctx", None),
    )
    out_specs = (P("dp", None, "ctx"), P("dp", None, "ctx"), P("dp", None, "ctx"), P("ctx", "dp"))
    return jax.shard_map(local, mesh=mesh, in_specs=in_specs, out_specs=out_specs, check_vma=False)
```

```python
import functools
import math

import jax
import jax.numpy as jnp
import numpy as np
from jax import lax
from jax.experimental import pallas as pl
from jax.experimental.pallas import tpu as pltpu
from jax.sharding import PartitionSpec as P

BLOCK = 128
bf16 = jnp.bfloat16
f32 = jnp.float32


def split_table(table):
    high = table.astype(bf16)
    return high, (table - high.astype(np.float64)).astype(bf16)


def make_tables(half, seq):
    length = 2 * seq
    k = np.arange(half) + 0.5
    first = 2.0 * math.pi * np.outer(k, np.arange(half)) / (2 * half)
    turn = 2.0 * math.pi * np.outer(k, np.arange(BLOCK)) / length
    block = 2.0 * math.pi * np.outer(np.arange(BLOCK), np.arange(BLOCK)) / BLOCK
    first_high, first_low = split_table(np.concatenate([np.cos(first), -np.sin(first)], 0))
    last_high, last_low = split_table(
        np.concatenate([np.cos(first).T, -np.sin(first).T], 1) * (2.0 / length)
    )
    cos, sin = np.cos(block), np.sin(block)
    mid_high, mid_low = split_table(np.block([[cos, -sin], [sin, cos]]))
    return {
        "forward": np.concatenate([first_high, first_high, first_low], 1),
        "back": np.concatenate([last_high, last_high, last_low], 1),
        "middle": np.concatenate([mid_high, mid_high, mid_low], 0),
        "turn": np.stack([np.cos(turn), np.sin(turn)]).astype(np.float32),
    }


def split(value):
    high = value.astype(bf16)
    return high, (value - high.astype(f32)).astype(bf16)


def dot(left, right):
    return jnp.dot(left, right, preferred_element_type=f32)


def middle_transform(rows, middle_ref):
    high, low = split(rows)
    return dot(jnp.concatenate([high, low, high], 1), middle_ref[...])


def forward_rows(rows_ref, chans, half, exact, forward_ref, turn_ref, middle_ref):
    cols = jnp.concatenate([rows_ref[pl.ds(c, half, stride=chans), :] for c in range(chans)], 1)
    if exact:
        high = cols.astype(bf16)
        table = jnp.concatenate([forward_ref[:, :half], forward_ref[:, 2 * half :]], 1)
        section = dot(table, jnp.concatenate([high, high], 0))
    else:
        high, low = split(cols)
        section = dot(forward_ref[...], jnp.concatenate([high, low, high], 0))
    cos, sin = turn_ref[0], turn_ref[1]
    rows = []
    for c in range(chans):
        re = section[:half, c * BLOCK : (c + 1) * BLOCK]
        im = section[half:, c * BLOCK : (c + 1) * BLOCK]
        rows.append(jnp.concatenate([re * cos + im * sin, im * cos - re * sin], 1))
    return middle_transform(jnp.concatenate(rows, 0), middle_ref)


def inverse_rows(spec, chans, half, out_ref, back_ref, turn_ref, middle_ref):
    inner = middle_transform(spec, middle_ref)
    cos, sin = turn_ref[0], turn_ref[1]
    cols = []
    for c in range(chans):
        re = inner[c * half : (c + 1) * half, :BLOCK]
        minus = inner[c * half : (c + 1) * half, BLOCK:]
        cols.append(jnp.concatenate([re * cos + minus * sin, re * sin - minus * cos], 0))
    high, low = split(jnp.concatenate(cols, 1))
    signal = dot(back_ref[...], jnp.concatenate([high, low, high], 0))
    for c in range(chans):
        out_ref[pl.ds(c, half, stride=chans), :] = signal[:, c * BLOCK : (c + 1) * BLOCK]


def gate_kernel(key_hbm, value_hbm, grad_hbm, query_hbm, out_ref, held, sems):
    groups, both, _ = out_ref.shape
    pieces = sems.shape[1]
    rows = key_hbm.shape[0] // pieces
    part = groups // pieces

    def copy(i, p):
        span = pl.ds(p * rows, rows)
        source = (key_hbm, value_hbm, grad_hbm, query_hbm)[i]
        return pltpu.make_async_copy(source.at[span, :], held.at[i, span, :], sems.at[i, p])

    for p in range(pieces):
        for i in range(4):
            copy(i, p).start()
    for p in range(pieces):
        for i in range(4):
            copy(i, p).wait()
        span = pl.ds(p * rows, rows)
        key, value, grad, query = (held[i, span, :].astype(f32) for i in range(4))
        shape = (part, both // 2, BLOCK)
        kv, dz = (key * value).reshape(shape), (grad * query).reshape(shape)
        out_ref[pl.ds(p * part, part)] = jnp.concatenate([kv, dz], 1).astype(bf16)


def filter_kernel(filter_ref, forward_ref, turn_ref, middle_ref, spec_ref, rows):
    chans, seq = filter_ref.shape
    half = seq // BLOCK
    for a in range(half):
        rows[pl.ds(a * chans, chans), :] = filter_ref[:, a * BLOCK : (a + 1) * BLOCK]
    spec_ref[...] = forward_rows(rows, chans, half, False, forward_ref, turn_ref, middle_ref)


def forward_kernel(both_ref, forward_ref, turn_ref, middle_ref, spec_ref, rows):
    half, both, _ = both_ref.shape
    rows[...] = both_ref[...].astype(f32).reshape(half * both, BLOCK)
    spec_ref[...] = forward_rows(rows, both, half, True, forward_ref, turn_ref, middle_ref)


def cross_kernel(
    spec_ref, after_ref, back_ref, turn_ref, middle_ref, keep_ref, send_ref, out_rows
):
    quads, own, chans, _ = keep_ref.shape
    half = quads * 2 * own
    count = chans * half
    kv_re, kv_im = spec_ref[:count, :BLOCK], spec_ref[:count, BLOCK:]
    dz_re, dz_im = spec_ref[count:, :BLOCK], spec_ref[count:, BLOCK:]
    cross = jnp.concatenate([kv_re * dz_re + kv_im * dz_im, kv_im * dz_re - kv_re * dz_im], 1)
    inverse_rows(cross, chans, half, out_rows, back_ref, turn_ref, middle_ref)
    core = lax.rem(lax.axis_index("dp"), 2)
    size = own * chans
    for z in range(quads):
        kept = pl.multiple_of((2 * z + core) * size, size)
        sent = pl.multiple_of((2 * z + 1 - core) * size, size)
        keep_ref[z] = out_rows[pl.ds(kept, size), :].reshape(own, chans, BLOCK)
        send_ref[z] = out_rows[pl.ds(sent, size), :].reshape(own, chans, BLOCK).astype(bf16)


def halve_kernel(keep_ref, other_ref, mine_ref, send_ref, *, step):
    z = lax.div(lax.axis_index("dp"), 2)
    bit = lax.rem(lax.div(z, step), 2)
    count = mine_ref.shape[0]
    mine, theirs = bit * count, (1 - bit) * count
    mine_ref[...] = keep_ref[pl.ds(mine, count)] + other_ref[pl.ds(mine, count)].astype(f32)
    send_ref[...] = (
        keep_ref[pl.ds(theirs, count)] + other_ref[pl.ds(theirs, count)].astype(f32)
    ).astype(bf16)


def conv_kernel(spec_ref, filter_ref, back_ref, turn_ref, middle_ref, out_ref, out_rows):
    half, both, _ = out_ref.shape
    count = half * both // 2
    f_re, f_im = filter_ref[:, :BLOCK], filter_ref[:, BLOCK:]
    kv_re, kv_im = spec_ref[:count, :BLOCK], spec_ref[:count, BLOCK:]
    dz_re, dz_im = spec_ref[count:, :BLOCK], spec_ref[count:, BLOCK:]
    conv = jnp.concatenate([f_re * kv_re - f_im * kv_im, -f_re * kv_im - f_im * kv_re], 1)
    dkv = jnp.concatenate([f_re * dz_re + f_im * dz_im, f_im * dz_re - f_re * dz_im], 1)
    inverse_rows(
        jnp.concatenate([conv, dkv], 0), both, half, out_rows, back_ref, turn_ref, middle_ref
    )
    out_ref[...] = out_rows[...].reshape(half, both, BLOCK).astype(bf16)


def final_kernel(both_ref, key_ref, value_ref, grad_ref, gq_ref, gk_ref, gv_ref):
    groups, both, _ = both_ref.shape
    chans = both // 2
    wide = both_ref[...].astype(f32)
    conv = wide[:, :chans, :].reshape(groups * chans, BLOCK)
    dkv = wide[:, chans:, :].reshape(groups * chans, BLOCK)
    gq_ref[...] = (grad_ref[...].astype(f32) * conv).astype(bf16)
    gk_ref[...] = (dkv * value_ref[...].astype(f32)).astype(bf16)
    gv_ref[...] = (dkv * key_ref[...].astype(f32)).astype(bf16)


def lag_kernel(keep_ref, other_ref, out_ref, *, scale):
    total = (keep_ref[0] + other_ref[0].astype(f32)) * scale
    for a in range(total.shape[0]):
        out_ref[:, a * BLOCK : (a + 1) * BLOCK] = total[a]


def call(kernel, out, *args, scratch=(), flops=0, name=None):
    nbytes = sum(math.prod(a.shape) * a.dtype.itemsize for a in args)
    vmem = pl.BlockSpec(memory_space=pltpu.VMEM)
    return pl.pallas_call(
        kernel,
        out_shape=out,
        in_specs=[vmem] * len(args),
        out_specs=jax.tree.map(lambda _: vmem, out),
        scratch_shapes=[pltpu.VMEM(shape, f32) for shape in scratch],
        compiler_params=pltpu.CompilerParams(vmem_limit_bytes=40 * 2**20),
        cost_estimate=pl.CostEstimate(flops=flops, bytes_accessed=nbytes, transcendentals=0),
        name=name,
    )(*args)


def local(query_gate, key_gate, value_gate, grad_out, long_filter):
    chans, seq = long_filter.shape
    half = seq // BLOCK
    groups = lax.axis_size("dp")
    total = query_gate.shape[1]
    both = 2 * chans
    tables = {name: jnp.asarray(table) for name, table in make_tables(half, seq).items()}
    forward, back = tables["forward"], tables["back"]
    turn, middle = tables["turn"], tables["middle"]
    query, key, value, grad = (
        x.reshape(total, BLOCK) for x in (query_gate, key_gate, value_gate, grad_out)
    )
    shape = jax.ShapeDtypeStruct
    pieces = shape((half, both, BLOCK), bf16)
    work = 2 * chans * half * 256 * 768

    gated = pl.pallas_call(
        gate_kernel,
        out_shape=pieces,
        in_specs=[pl.BlockSpec(memory_space=pltpu.HBM)] * 4,
        out_specs=pl.BlockSpec(memory_space=pltpu.VMEM),
        scratch_shapes=[
            pltpu.VMEM((4, total, BLOCK), bf16),
            pltpu.SemaphoreType.DMA((4, 4)),
        ],
        compiler_params=pltpu.CompilerParams(vmem_limit_bytes=63 * 2**20),
        cost_estimate=pl.CostEstimate(
            flops=total * BLOCK * 2, bytes_accessed=total * BLOCK * 12, transcendentals=0
        ),
        name="gate",
    )(key, value, grad, query)
    here = lax.all_to_all(gated, "ctx", 0, 0, tiled=True)
    filter_spec = call(
        filter_kernel,
        shape((chans * half, 2 * BLOCK), f32),
        long_filter,
        forward,
        turn,
        middle,
        scratch=[(half * chans, BLOCK)],
        flops=2 * work,
        name="filter",
    )
    spec = call(
        forward_kernel,
        shape((both * half, 2 * BLOCK), f32),
        here,
        forward,
        turn,
        middle,
        scratch=[(half * both, BLOCK)],
        flops=3 * work,
        name="forward",
    )
    carried = call(
        conv_kernel,
        pieces,
        spec,
        filter_spec,
        back,
        turn,
        middle,
        scratch=[(half * both, BLOCK)],
        flops=4 * work,
        name="conv",
    )
    back_here = lax.all_to_all(carried, "ctx", 0, 0, tiled=True)
    own = half // groups
    quads = groups // 2
    quad = (own, chans, BLOCK)
    keep, send = call(
        cross_kernel,
        (shape((quads, *quad), f32), shape((quads, *quad), bf16)),
        spec,
        carried,
        back,
        turn,
        middle,
        scratch=[(half * chans, BLOCK)],
        flops=2 * work,
        name="cross",
    )
    other = lax.ppermute(send, "dp", [(i, i ^ 1) for i in range(groups)])
    step = quads // 2
    while step:
        keep, send = call(
            functools.partial(halve_kernel, step=step),
            (shape((step, *quad), f32), shape((step, *quad), bf16)),
            keep,
            other,
            name="halve",
        )
        other = lax.ppermute(send, "dp", [(i, i ^ (2 * step)) for i in range(groups)])
        step //= 2
    grad_filter = call(
        lambda *refs: lag_kernel(*refs, scale=1.0 / math.sqrt(seq * groups)),
        shape((chans, own * BLOCK), f32),
        keep,
        other,
        name="lag_sum",
    )
    grads = call(
        final_kernel,
        (shape((total, BLOCK), bf16),) * 3,
        back_here,
        key,
        value,
        grad,
        name="final",
    )
    return tuple(g[None] for g in grads) + (grad_filter,)


def solution(mesh):
    in_specs = (
        P("dp", None, "ctx"),
        P("dp", None, "ctx"),
        P("dp", None, "ctx"),
        P("dp", None, "ctx"),
        P("ctx", None),
    )
    out_specs = (P("dp", None, "ctx"), P("dp", None, "ctx"), P("dp", None, "ctx"), P("ctx", "dp"))
    return jax.shard_map(local, mesh=mesh, in_specs=in_specs, out_specs=out_specs, check_vma=False)
```

```python
import functools
import math

import jax
import jax.numpy as jnp
import numpy as np
from jax import lax
from jax.experimental import pallas as pl
from jax.experimental.pallas import tpu as pltpu
from jax.sharding import PartitionSpec as P

BLOCK = 128
bf16 = jnp.bfloat16
f32 = jnp.float32


FAR_IN, FAR_OUT = 58, 58
HINT = 30 * 10**9


def slots(count, far):
    return [m ^ far for m in range(count)]


def swap_slots(blocks, far):
    rest = blocks.shape[1:]
    for bit in (1 << b for b in range(6)):
        if far & bit and bit < blocks.shape[0]:
            pairs = blocks.reshape(blocks.shape[0] // (2 * bit), 2, bit, *rest)
            blocks = jnp.concatenate([pairs[:, 1:], pairs[:, :1]], 1).reshape(-1, *rest)
    return blocks


def split_table(table):
    high = table.astype(bf16)
    return high, (table - high.astype(np.float64)).astype(bf16)


def make_tables(half, seq):
    length = 2 * seq
    k = np.arange(half) + 0.5
    first = 2.0 * math.pi * np.outer(k, np.arange(half)) / (2 * half)
    turn = 2.0 * math.pi * np.outer(k, np.arange(BLOCK)) / length
    block = 2.0 * math.pi * np.outer(np.arange(BLOCK), np.arange(BLOCK)) / BLOCK
    came = slots(half, FAR_IN)
    first_high, first_low = split_table(np.concatenate([np.cos(first), -np.sin(first)], 0)[:, came])
    last_high, last_low = split_table(
        np.concatenate([np.cos(first).T, -np.sin(first).T], 1) * (2.0 / length)
    )
    back = np.concatenate([last_high, last_high, last_low], 1)
    cos, sin = np.cos(block), np.sin(block)
    mid_high, mid_low = split_table(np.block([[cos, -sin], [sin, cos]]))
    return {
        "forward": np.concatenate([first_high, first_high, first_low], 1),
        "back": back[slots(half, FAR_OUT)],
        "lag": back,
        "middle": np.concatenate([mid_high, mid_high, mid_low], 0),
        "turn": np.stack([np.cos(turn), np.sin(turn)]).astype(np.float32),
    }


def split(value):
    high = value.astype(bf16)
    return high, (value - high.astype(f32)).astype(bf16)


def dot(left, right):
    return jnp.dot(left, right, preferred_element_type=f32)


def middle_transform(rows, middle_ref):
    high, low = split(rows)
    return dot(jnp.concatenate([high, low, high], 1), middle_ref[...])


def forward_rows(rows_ref, chans, half, exact, forward_ref, turn_ref, middle_ref):
    cols = jnp.concatenate([rows_ref[pl.ds(c, half, stride=chans), :] for c in range(chans)], 1)
    if exact:
        high = cols.astype(bf16)
        table = jnp.concatenate([forward_ref[:, :half], forward_ref[:, 2 * half :]], 1)
        section = dot(table, jnp.concatenate([high, high], 0))
    else:
        high, low = split(cols)
        section = dot(forward_ref[...], jnp.concatenate([high, low, high], 0))
    cos, sin = turn_ref[0], turn_ref[1]
    rows = []
    for c in range(chans):
        re = section[:half, c * BLOCK : (c + 1) * BLOCK]
        im = section[half:, c * BLOCK : (c + 1) * BLOCK]
        rows.append(jnp.concatenate([re * cos + im * sin, im * cos - re * sin], 1))
    return middle_transform(jnp.concatenate(rows, 0), middle_ref)


def inverse_rows(spec, chans, half, out_ref, back_ref, turn_ref, middle_ref):
    inner = middle_transform(spec, middle_ref)
    cos, sin = turn_ref[0], turn_ref[1]
    cols = []
    for c in range(chans):
        re = inner[c * half : (c + 1) * half, :BLOCK]
        minus = inner[c * half : (c + 1) * half, BLOCK:]
        cols.append(jnp.concatenate([re * cos + minus * sin, re * sin - minus * cos], 0))
    high, low = split(jnp.concatenate(cols, 1))
    signal = dot(back_ref[...], jnp.concatenate([high, low, high], 0))
    for c in range(chans):
        out_ref[pl.ds(c, half, stride=chans), :] = signal[:, c * BLOCK : (c + 1) * BLOCK]


def gate_kernel(key_hbm, value_hbm, grad_hbm, query_hbm, out_ref, held, sems):
    groups, both, _ = out_ref.shape
    pieces = sems.shape[1]
    rows = key_hbm.shape[0] // pieces
    part = groups // pieces

    def copy(i, p):
        span = pl.ds(p * rows, rows)
        source = (key_hbm, value_hbm, grad_hbm, query_hbm)[i]
        return pltpu.make_async_copy(source.at[span, :], held.at[i, span, :], sems.at[i, p])

    for p in range(pieces):
        for i in range(4):
            copy(i, p).start()
    for p in range(pieces):
        for i in range(4):
            copy(i, p).wait()
        span = pl.ds(p * rows, rows)
        key, value, grad, query = (held[i, span, :].astype(f32) for i in range(4))
        shape = (part, both // 2, BLOCK)
        kv, dz = (key * value).reshape(shape), (grad * query).reshape(shape)
        to = (p * part ^ FAR_IN) // part * part
        out_ref[pl.ds(to, part)] = swap_slots(jnp.concatenate([kv, dz], 1).astype(bf16), FAR_IN)


def filter_kernel(filter_ref, forward_ref, turn_ref, middle_ref, spec_ref, rows):
    chans, seq = filter_ref.shape
    half = seq // BLOCK
    for a, slot in enumerate(slots(half, FAR_IN)):
        rows[pl.ds(slot * chans, chans), :] = filter_ref[:, a * BLOCK : (a + 1) * BLOCK]
    spec_ref[...] = forward_rows(rows, chans, half, False, forward_ref, turn_ref, middle_ref)


def forward_kernel(both_ref, forward_ref, turn_ref, middle_ref, spec_ref, rows):
    half, both, _ = both_ref.shape
    rows[...] = both_ref[...].astype(f32).reshape(half * both, BLOCK)
    spec_ref[...] = forward_rows(rows, both, half, True, forward_ref, turn_ref, middle_ref)


def cross_kernel(spec_ref, back_ref, turn_ref, middle_ref, keep_ref, send_ref, out_rows):
    pairs, cores, own, chans, _ = keep_ref.shape
    half = 2 * pairs * cores * own
    count = chans * half
    kv_re, kv_im = spec_ref[:count, :BLOCK], spec_ref[:count, BLOCK:]
    dz_re, dz_im = spec_ref[count:, :BLOCK], spec_ref[count:, BLOCK:]
    cross = jnp.concatenate([kv_re * dz_re + kv_im * dz_im, kv_im * dz_re - kv_re * dz_im], 1)
    inverse_rows(cross, chans, half, out_rows, back_ref, turn_ref, middle_ref)
    bit = lax.div(lax.axis_index("dp"), 4)
    size = out_rows.shape[0] // 2
    kept = pl.multiple_of(bit * size, size)
    sent = pl.multiple_of((1 - bit) * size, size)
    keep_ref[...] = out_rows[pl.ds(kept, size), :].reshape(keep_ref.shape)
    send_ref[...] = out_rows[pl.ds(sent, size), :].reshape(send_ref.shape).astype(bf16)


def halve_kernel(keep_ref, other_ref, mine_ref, send_ref, *, axis_bit):
    bit = lax.rem(lax.div(lax.axis_index("dp"), axis_bit), 2)
    mine_ref[...] = keep_ref[bit] + other_ref[bit].astype(f32)
    send_ref[...] = (keep_ref[1 - bit] + other_ref[1 - bit].astype(f32)).astype(bf16)


def conv_kernel(spec_ref, filter_ref, back_ref, turn_ref, middle_ref, after_ref, out_ref, out_rows):
    half, both, _ = out_ref.shape
    count = half * both // 2
    f_re, f_im = filter_ref[:, :BLOCK], filter_ref[:, BLOCK:]
    kv_re, kv_im = spec_ref[:count, :BLOCK], spec_ref[:count, BLOCK:]
    dz_re, dz_im = spec_ref[count:, :BLOCK], spec_ref[count:, BLOCK:]
    conv = jnp.concatenate([f_re * kv_re - f_im * kv_im, -f_re * kv_im - f_im * kv_re], 1)
    dkv = jnp.concatenate([f_re * dz_re + f_im * dz_im, f_im * dz_re - f_re * dz_im], 1)
    inverse_rows(
        jnp.concatenate([conv, dkv], 0), both, half, out_rows, back_ref, turn_ref, middle_ref
    )
    out_ref[...] = out_rows[...].reshape(half, both, BLOCK).astype(bf16)


def final_kernel(
    both_ref,
    key_ref,
    value_ref,
    grad_ref,
    keep_ref,
    other_ref,
    gq_ref,
    gk_ref,
    gv_ref,
    gf_ref,
    *,
    scale,
):
    core = lax.rem(lax.axis_index("dp"), 2)
    lags = (keep_ref[...] + other_ref[1 - core].astype(f32)) * scale
    for a in range(lags.shape[0]):
        gf_ref[:, a * BLOCK : (a + 1) * BLOCK] = lags[a]
    groups, both, _ = both_ref.shape
    chans = both // 2
    wide = swap_slots(both_ref[...], FAR_OUT).astype(f32)
    conv = wide[:, :chans, :].reshape(groups * chans, BLOCK)
    dkv = wide[:, chans:, :].reshape(groups * chans, BLOCK)
    gq_ref[...] = (grad_ref[...].astype(f32) * conv).astype(bf16)
    gk_ref[...] = (dkv * value_ref[...].astype(f32)).astype(bf16)
    gv_ref[...] = (dkv * key_ref[...].astype(f32)).astype(bf16)


def call(kernel, out, *args, scratch=(), flops=0, any_space=0, name=None):
    nbytes = sum(math.prod(a.shape) * a.dtype.itemsize for a in args)
    vmem = pl.BlockSpec(memory_space=pltpu.VMEM)
    return pl.pallas_call(
        kernel,
        out_shape=out,
        in_specs=[vmem] * (len(args) - any_space)
        + [pl.BlockSpec(memory_space=pl.ANY)] * any_space,
        out_specs=jax.tree.map(lambda _: vmem, out),
        scratch_shapes=[pltpu.VMEM(shape, f32) for shape in scratch],
        compiler_params=pltpu.CompilerParams(vmem_limit_bytes=40 * 2**20),
        cost_estimate=pl.CostEstimate(flops=flops, bytes_accessed=nbytes, transcendentals=0),
        name=name,
    )(*args)


def local(query_gate, key_gate, value_gate, grad_out, long_filter):
    chans, seq = long_filter.shape
    half = seq // BLOCK
    groups = lax.axis_size("dp")
    total = query_gate.shape[1]
    both = 2 * chans
    tables = {name: jnp.asarray(table) for name, table in make_tables(half, seq).items()}
    forward, back = tables["forward"], tables["back"]
    turn, middle, lag_back = tables["turn"], tables["middle"], tables["lag"]
    query, key, value, grad = (
        x.reshape(total, BLOCK) for x in (query_gate, key_gate, value_gate, grad_out)
    )
    shape = jax.ShapeDtypeStruct
    pieces = shape((half, both, BLOCK), bf16)
    work = 2 * chans * half * 256 * 768

    gated = pl.pallas_call(
        gate_kernel,
        out_shape=pieces,
        in_specs=[pl.BlockSpec(memory_space=pltpu.HBM)] * 4,
        out_specs=pl.BlockSpec(memory_space=pltpu.VMEM),
        scratch_shapes=[
            pltpu.VMEM((4, total, BLOCK), bf16),
            pltpu.SemaphoreType.DMA((4, 4)),
        ],
        compiler_params=pltpu.CompilerParams(vmem_limit_bytes=63 * 2**20),
        cost_estimate=pl.CostEstimate(
            flops=total * BLOCK * 2, bytes_accessed=total * BLOCK * 12, transcendentals=0
        ),
        name="gate",
    )(key, value, grad, query)
    here = lax.all_to_all(
        gated, "ctx", 0, 0, tiled=True, axis_index_groups=[slots(half, FAR_IN)]
    )
    filter_spec = call(
        filter_kernel,
        shape((chans * half, 2 * BLOCK), f32),
        long_filter,
        forward,
        turn,
        middle,
        scratch=[(half * chans, BLOCK)],
        flops=2 * work,
        name="filter",
    )
    spec = call(
        forward_kernel,
        shape((both * half, 2 * BLOCK), f32),
        here,
        forward,
        turn,
        middle,
        scratch=[(half * both, BLOCK)],
        flops=3 * work,
        name="forward",
    )
    own = half // groups
    quads = groups // 2
    quad = (own, chans, BLOCK)
    keep, send = call(
        cross_kernel,
        (shape((2, 2, *quad), f32), shape((2, 2, *quad), bf16)),
        spec,
        lag_back,
        turn,
        middle,
        scratch=[(half * chans, BLOCK)],
        flops=2 * work,
        name="cross",
    )
    other = lax.ppermute(send, "dp", [(i, i ^ 4) for i in range(groups)])
    carried = call(
        conv_kernel,
        pieces,
        spec,
        filter_spec,
        back,
        turn,
        middle,
        send,
        scratch=[(half * both, BLOCK)],
        flops=4 * work,
        any_space=1,
        name="conv",
    )
    keep, send = call(
        functools.partial(halve_kernel, axis_bit=2),
        (shape((2, *quad), f32), shape((2, *quad), bf16)),
        keep,
        other,
        flops=HINT,
        name="halve",
    )
    other = lax.ppermute(send, "dp", [(i, i ^ 2) for i in range(groups)])
    keep, send = call(
        functools.partial(halve_kernel, axis_bit=1),
        (shape(quad, f32), shape(quad, bf16)),
        keep,
        other,
        name="pair",
    )
    cores = [[2 * z, 2 * z + 1] for z in range(quads)]
    other = lax.all_gather(send, "dp", axis=0, axis_index_groups=cores)
    back_here = lax.all_to_all(
        carried, "ctx", 0, 0, tiled=True, axis_index_groups=[slots(half, FAR_OUT)]
    )
    *grads, grad_filter = call(
        functools.partial(final_kernel, scale=1.0 / math.sqrt(seq * groups)),
        (shape((total, BLOCK), bf16),) * 3 + (shape((chans, own * BLOCK), f32),),
        back_here,
        key,
        value,
        grad,
        keep,
        other,
        name="final",
    )
    return tuple(g[None] for g in grads) + (grad_filter,)


def solution(mesh):
    in_specs = (
        P("dp", None, "ctx"),
        P("dp", None, "ctx"),
        P("dp", None, "ctx"),
        P("dp", None, "ctx"),
        P("ctx", None),
    )
    out_specs = (P("dp", None, "ctx"), P("dp", None, "ctx"), P("dp", None, "ctx"), P("ctx", "dp"))
    return jax.shard_map(local, mesh=mesh, in_specs=in_specs, out_specs=out_specs, check_vma=False)
```

```python
import functools
import math

import jax
import jax.numpy as jnp
import numpy as np
from jax import lax
from jax.experimental import pallas as pl
from jax.experimental.pallas import tpu as pltpu
from jax.sharding import PartitionSpec as P

BLOCK = 128
bf16 = jnp.bfloat16
f32 = jnp.float32


FAR_IN, FAR_OUT = 58, 58
HINT = 30 * 10**9


def slots(count, far):
    return [m ^ far for m in range(count)]


def swap_slots(blocks, far):
    rest = blocks.shape[1:]
    for bit in (1 << b for b in range(6)):
        if far & bit and bit < blocks.shape[0]:
            pairs = blocks.reshape(blocks.shape[0] // (2 * bit), 2, bit, *rest)
            blocks = jnp.concatenate([pairs[:, 1:], pairs[:, :1]], 1).reshape(-1, *rest)
    return blocks


def split_table(table):
    high = table.astype(bf16)
    return high, (table - high.astype(np.float64)).astype(bf16)


def make_tables(half, seq):
    length = 2 * seq
    k = np.arange(half) + 0.5
    first = 2.0 * math.pi * np.outer(k, np.arange(half)) / (2 * half)
    turn = 2.0 * math.pi * np.outer(k, np.arange(BLOCK)) / length
    block = 2.0 * math.pi * np.outer(np.arange(BLOCK), np.arange(BLOCK)) / BLOCK
    came = slots(half, FAR_IN)
    first_high, first_low = split_table(np.concatenate([np.cos(first), -np.sin(first)], 0)[:, came])
    back = np.concatenate([np.cos(first).T, -np.sin(first).T], 1) * (2.0 / length)
    back = back.astype(bf16)
    cos, sin = np.cos(block), np.sin(block)
    mid_high, mid_low = split_table(np.block([[cos, -sin], [sin, cos]]))
    return {
        "forward": np.concatenate([first_high, first_high, first_low], 1),
        "back": back[slots(half, FAR_OUT)],
        "lag": back,
        "middle": np.concatenate([mid_high, mid_high, mid_low], 0),
        "turn": np.stack([np.cos(turn), np.sin(turn)]).astype(np.float32),
    }


def split(value):
    high = value.astype(bf16)
    return high, (value - high.astype(f32)).astype(bf16)


def dot(left, right):
    return jnp.dot(left, right, preferred_element_type=f32)


def middle_exact(rows, middle_ref):
    high, low = split(rows)
    return dot(jnp.concatenate([high, low, high], 1), middle_ref[...])


def forward_rows(rows_ref, chans, half, exact, forward_ref, turn_ref, middle_ref):
    cols = jnp.concatenate([rows_ref[pl.ds(c, half, stride=chans), :] for c in range(chans)], 1)
    if exact:
        high = cols.astype(bf16)
        table = jnp.concatenate([forward_ref[:, :half], forward_ref[:, 2 * half :]], 1)
        section = dot(table, jnp.concatenate([high, high], 0))
    else:
        high, low = split(cols)
        section = dot(forward_ref[...], jnp.concatenate([high, low, high], 0))
    cos, sin = turn_ref[0], turn_ref[1]
    rows = []
    for c in range(chans):
        re = section[:half, c * BLOCK : (c + 1) * BLOCK]
        im = section[half:, c * BLOCK : (c + 1) * BLOCK]
        rows.append(jnp.concatenate([re * cos + im * sin, im * cos - re * sin], 1))
    return middle_exact(jnp.concatenate(rows, 0), middle_ref)


def inverse_rows(spec, chans, half, out_ref, back_ref, turn_ref, middle_ref):
    inner = dot(spec.astype(bf16), middle_ref[: 2 * BLOCK, :])
    cos, sin = turn_ref[0], turn_ref[1]
    cols = []
    for c in range(chans):
        re = inner[c * half : (c + 1) * half, :BLOCK]
        minus = inner[c * half : (c + 1) * half, BLOCK:]
        cols.append(jnp.concatenate([re * cos + minus * sin, re * sin - minus * cos], 0))
    signal = dot(back_ref[...], jnp.concatenate(cols, 1).astype(bf16))
    for c in range(chans):
        out_ref[pl.ds(c, half, stride=chans), :] = signal[:, c * BLOCK : (c + 1) * BLOCK]


def gate_kernel(key_hbm, value_hbm, grad_hbm, query_hbm, out_ref, held, sems):
    groups, both, _ = out_ref.shape
    pieces = sems.shape[1]
    rows = key_hbm.shape[0] // pieces
    part = groups // pieces

    def copy(i, p):
        span = pl.ds(p * rows, rows)
        source = (key_hbm, value_hbm, grad_hbm, query_hbm)[i]
        return pltpu.make_async_copy(source.at[span, :], held.at[i, span, :], sems.at[i, p])

    for p in range(pieces):
        for i in range(4):
            copy(i, p).start()
    for p in range(pieces):
        for i in range(4):
            copy(i, p).wait()
        span = pl.ds(p * rows, rows)
        key, value, grad, query = (held[i, span, :].astype(f32) for i in range(4))
        shape = (part, both // 2, BLOCK)
        kv, dz = (key * value).reshape(shape), (grad * query).reshape(shape)
        to = (p * part ^ FAR_IN) // part * part
        out_ref[pl.ds(to, part)] = swap_slots(jnp.concatenate([kv, dz], 1).astype(bf16), FAR_IN)


def filter_kernel(filter_ref, forward_ref, turn_ref, middle_ref, spec_ref, rows):
    chans, seq = filter_ref.shape
    half = seq // BLOCK
    for a, slot in enumerate(slots(half, FAR_IN)):
        rows[pl.ds(slot * chans, chans), :] = filter_ref[:, a * BLOCK : (a + 1) * BLOCK]
    spec_ref[...] = forward_rows(rows, chans, half, False, forward_ref, turn_ref, middle_ref)


def forward_kernel(both_ref, forward_ref, turn_ref, middle_ref, spec_ref, rows):
    half, both, _ = both_ref.shape
    rows[...] = both_ref[...].astype(f32).reshape(half * both, BLOCK)
    spec_ref[...] = forward_rows(rows, both, half, True, forward_ref, turn_ref, middle_ref)


def cross_kernel(spec_ref, back_ref, turn_ref, middle_ref, keep_ref, send_ref, out_rows):
    pairs, cores, own, chans, _ = keep_ref.shape
    half = 2 * pairs * cores * own
    count = chans * half
    kv_re, kv_im = spec_ref[:count, :BLOCK], spec_ref[:count, BLOCK:]
    dz_re, dz_im = spec_ref[count:, :BLOCK], spec_ref[count:, BLOCK:]
    cross = jnp.concatenate([kv_re * dz_re + kv_im * dz_im, kv_im * dz_re - kv_re * dz_im], 1)
    inverse_rows(cross, chans, half, out_rows, back_ref, turn_ref, middle_ref)
    bit = lax.div(lax.axis_index("dp"), 4)
    size = out_rows.shape[0] // 2
    kept = pl.multiple_of(bit * size, size)
    sent = pl.multiple_of((1 - bit) * size, size)
    keep_ref[...] = out_rows[pl.ds(kept, size), :].reshape(keep_ref.shape)
    send_ref[...] = out_rows[pl.ds(sent, size), :].reshape(send_ref.shape).astype(bf16)


def halve_kernel(keep_ref, other_ref, mine_ref, send_ref, *, axis_bit):
    bit = lax.rem(lax.div(lax.axis_index("dp"), axis_bit), 2)
    mine_ref[...] = keep_ref[bit] + other_ref[bit].astype(f32)
    send_ref[...] = (keep_ref[1 - bit] + other_ref[1 - bit].astype(f32)).astype(bf16)


def conv_kernel(spec_ref, filter_ref, back_ref, turn_ref, middle_ref, after_ref, out_ref, out_rows):
    half, both, _ = out_ref.shape
    count = half * both // 2
    f_re, f_im = filter_ref[:, :BLOCK], filter_ref[:, BLOCK:]
    kv_re, kv_im = spec_ref[:count, :BLOCK], spec_ref[:count, BLOCK:]
    dz_re, dz_im = spec_ref[count:, :BLOCK], spec_ref[count:, BLOCK:]
    conv = jnp.concatenate([f_re * kv_re - f_im * kv_im, -f_re * kv_im - f_im * kv_re], 1)
    dkv = jnp.concatenate([f_re * dz_re + f_im * dz_im, f_im * dz_re - f_re * dz_im], 1)
    inverse_rows(
        jnp.concatenate([conv, dkv], 0), both, half, out_rows, back_ref, turn_ref, middle_ref
    )
    out_ref[...] = out_rows[...].reshape(half, both, BLOCK).astype(bf16)


def final_kernel(
    both_ref,
    key_ref,
    value_ref,
    grad_ref,
    keep_ref,
    other_ref,
    gq_ref,
    gk_ref,
    gv_ref,
    gf_ref,
    *,
    scale,
):
    core = lax.rem(lax.axis_index("dp"), 2)
    lags = (keep_ref[...] + other_ref[1 - core].astype(f32)) * scale
    for a in range(lags.shape[0]):
        gf_ref[:, a * BLOCK : (a + 1) * BLOCK] = lags[a]
    groups, both, _ = both_ref.shape
    chans = both // 2
    wide = swap_slots(both_ref[...], FAR_OUT).astype(f32)
    conv = wide[:, :chans, :].reshape(groups * chans, BLOCK)
    dkv = wide[:, chans:, :].reshape(groups * chans, BLOCK)
    gq_ref[...] = (grad_ref[...].astype(f32) * conv).astype(bf16)
    gk_ref[...] = (dkv * value_ref[...].astype(f32)).astype(bf16)
    gv_ref[...] = (dkv * key_ref[...].astype(f32)).astype(bf16)


def call(kernel, out, *args, scratch=(), flops=0, any_space=0, name=None):
    nbytes = sum(math.prod(a.shape) * a.dtype.itemsize for a in args)
    vmem = pl.BlockSpec(memory_space=pltpu.VMEM)
    return pl.pallas_call(
        kernel,
        out_shape=out,
        in_specs=[vmem] * (len(args) - any_space)
        + [pl.BlockSpec(memory_space=pl.ANY)] * any_space,
        out_specs=jax.tree.map(lambda _: vmem, out),
        scratch_shapes=[pltpu.VMEM(shape, f32) for shape in scratch],
        compiler_params=pltpu.CompilerParams(vmem_limit_bytes=40 * 2**20),
        cost_estimate=pl.CostEstimate(flops=flops, bytes_accessed=nbytes, transcendentals=0),
        name=name,
    )(*args)


def local(query_gate, key_gate, value_gate, grad_out, long_filter):
    chans, seq = long_filter.shape
    half = seq // BLOCK
    groups = lax.axis_size("dp")
    total = query_gate.shape[1]
    both = 2 * chans
    tables = {name: jnp.asarray(table) for name, table in make_tables(half, seq).items()}
    forward, back = tables["forward"], tables["back"]
    turn, middle, lag_back = tables["turn"], tables["middle"], tables["lag"]
    query, key, value, grad = (
        x.reshape(total, BLOCK) for x in (query_gate, key_gate, value_gate, grad_out)
    )
    shape = jax.ShapeDtypeStruct
    pieces = shape((half, both, BLOCK), bf16)
    work = 2 * chans * half * 256 * 768

    gated = pl.pallas_call(
        gate_kernel,
        out_shape=pieces,
        in_specs=[pl.BlockSpec(memory_space=pltpu.HBM)] * 4,
        out_specs=pl.BlockSpec(memory_space=pltpu.VMEM),
        scratch_shapes=[
            pltpu.VMEM((4, total, BLOCK), bf16),
            pltpu.SemaphoreType.DMA((4, 4)),
        ],
        compiler_params=pltpu.CompilerParams(vmem_limit_bytes=63 * 2**20),
        cost_estimate=pl.CostEstimate(
            flops=total * BLOCK * 2, bytes_accessed=total * BLOCK * 12, transcendentals=0
        ),
        name="gate",
    )(key, value, grad, query)
    here = lax.all_to_all(
        gated, "ctx", 0, 0, tiled=True, axis_index_groups=[slots(half, FAR_IN)]
    )
    filter_spec = call(
        filter_kernel,
        shape((chans * half, 2 * BLOCK), f32),
        long_filter,
        forward,
        turn,
        middle,
        scratch=[(half * chans, BLOCK)],
        flops=2 * work,
        name="filter",
    )
    spec = call(
        forward_kernel,
        shape((both * half, 2 * BLOCK), f32),
        here,
        forward,
        turn,
        middle,
        scratch=[(half * both, BLOCK)],
        flops=3 * work,
        name="forward",
    )
    own = half // groups
    quads = groups // 2
    quad = (own, chans, BLOCK)
    keep, send = call(
        cross_kernel,
        (shape((2, 2, *quad), f32), shape((2, 2, *quad), bf16)),
        spec,
        lag_back,
        turn,
        middle,
        scratch=[(half * chans, BLOCK)],
        flops=2 * work,
        name="cross",
    )
    other = lax.ppermute(send, "dp", [(i, i ^ 4) for i in range(groups)])
    carried = call(
        conv_kernel,
        pieces,
        spec,
        filter_spec,
        back,
        turn,
        middle,
        send,
        scratch=[(half * both, BLOCK)],
        flops=4 * work,
        any_space=1,
        name="conv",
    )
    keep, send = call(
        functools.partial(halve_kernel, axis_bit=2),
        (shape((2, *quad), f32), shape((2, *quad), bf16)),
        keep,
        other,
        flops=HINT,
        name="halve",
    )
    other = lax.ppermute(send, "dp", [(i, i ^ 2) for i in range(groups)])
    keep, send = call(
        functools.partial(halve_kernel, axis_bit=1),
        (shape(quad, f32), shape(quad, bf16)),
        keep,
        other,
        name="pair",
    )
    cores = [[2 * z, 2 * z + 1] for z in range(quads)]
    other = lax.all_gather(send, "dp", axis=0, axis_index_groups=cores)
    back_here = lax.all_to_all(
        carried, "ctx", 0, 0, tiled=True, axis_index_groups=[slots(half, FAR_OUT)]
    )
    *grads, grad_filter = call(
        functools.partial(final_kernel, scale=1.0 / math.sqrt(seq * groups)),
        (shape((total, BLOCK), bf16),) * 3 + (shape((chans, own * BLOCK), f32),),
        back_here,
        key,
        value,
        grad,
        keep,
        other,
        name="final",
    )
    return tuple(g[None] for g in grads) + (grad_filter,)


def solution(mesh):
    in_specs = (
        P("dp", None, "ctx"),
        P("dp", None, "ctx"),
        P("dp", None, "ctx"),
        P("dp", None, "ctx"),
        P("ctx", None),
    )
    out_specs = (P("dp", None, "ctx"), P("dp", None, "ctx"), P("dp", None, "ctx"), P("ctx", "dp"))
    return jax.shard_map(local, mesh=mesh, in_specs=in_specs, out_specs=out_specs, check_vma=False)
```

```python
import functools
import math

import jax
import jax.numpy as jnp
import numpy as np
from jax import lax
from jax.experimental import pallas as pl
from jax.experimental.pallas import tpu as pltpu
from jax.sharding import PartitionSpec as P

BLOCK = 128
bf16 = jnp.bfloat16
f32 = jnp.float32


FAR_IN, FAR_OUT = 58, 58
HINT = 30 * 10**9


def slots(count, far):
    return [m ^ far for m in range(count)]


def swap_slots(blocks, far):
    rest = blocks.shape[1:]
    for bit in (1 << b for b in range(6)):
        if far & bit and bit < blocks.shape[0]:
            pairs = blocks.reshape(blocks.shape[0] // (2 * bit), 2, bit, *rest)
            blocks = jnp.concatenate([pairs[:, 1:], pairs[:, :1]], 1).reshape(-1, *rest)
    return blocks


def split_table(table):
    high = table.astype(bf16)
    return high, (table - high.astype(np.float64)).astype(bf16)


def make_tables(half, seq):
    length = 2 * seq
    k = np.arange(half) + 0.5
    first = 2.0 * math.pi * np.outer(k, np.arange(half)) / (2 * half)
    turn = 2.0 * math.pi * np.outer(k, np.arange(BLOCK)) / length
    block = 2.0 * math.pi * np.outer(np.arange(BLOCK), np.arange(BLOCK)) / BLOCK
    came = slots(half, FAR_IN)
    first_high, first_low = split_table(np.concatenate([np.cos(first), -np.sin(first)], 0)[:, came])
    back = np.concatenate([np.cos(first).T, -np.sin(first).T], 1) * (2.0 / length)
    back = back.astype(bf16)
    cos, sin = np.cos(block), np.sin(block)
    mid_high, mid_low = split_table(np.block([[cos, -sin], [sin, cos]]))
    return {
        "forward": np.concatenate([first_high, first_high, first_low], 1),
        "back": back[slots(half, FAR_OUT)],
        "lag": back,
        "middle": np.concatenate([mid_high, mid_high, mid_low], 0),
        "turn": np.stack([np.cos(turn), np.sin(turn)]).astype(np.float32),
    }


def split(value):
    high = value.astype(bf16)
    return high, (value - high.astype(f32)).astype(bf16)


def dot(left, right):
    return jnp.dot(left, right, preferred_element_type=f32)


def middle_exact(rows, middle_ref):
    high, low = split(rows)
    return dot(jnp.concatenate([high, low, high], 1), middle_ref[...])


def forward_rows(rows_ref, chans, half, exact, forward_ref, turn_ref, middle_ref):
    cols = jnp.concatenate([rows_ref[pl.ds(c, half, stride=chans), :] for c in range(chans)], 1)
    if exact:
        high = cols.astype(bf16)
        table = jnp.concatenate([forward_ref[:, :half], forward_ref[:, 2 * half :]], 1)
        section = dot(table, jnp.concatenate([high, high], 0))
    else:
        high, low = split(cols)
        section = dot(forward_ref[...], jnp.concatenate([high, low, high], 0))
    cos, sin = turn_ref[0], turn_ref[1]
    rows = []
    for c in range(chans):
        re = section[:half, c * BLOCK : (c + 1) * BLOCK]
        im = section[half:, c * BLOCK : (c + 1) * BLOCK]
        rows.append(jnp.concatenate([re * cos + im * sin, im * cos - re * sin], 1))
    return middle_exact(jnp.concatenate(rows, 0), middle_ref)


def inverse_rows(spec, chans, half, out_ref, back_ref, turn_ref, middle_ref):
    inner = dot(spec.astype(bf16), middle_ref[: 2 * BLOCK, :])
    cos, sin = turn_ref[0], turn_ref[1]
    cols = []
    for c in range(chans):
        re = inner[c * half : (c + 1) * half, :BLOCK]
        minus = inner[c * half : (c + 1) * half, BLOCK:]
        cols.append(jnp.concatenate([re * cos + minus * sin, re * sin - minus * cos], 0))
    signal = dot(back_ref[...], jnp.concatenate(cols, 1).astype(bf16))
    for c in range(chans):
        out_ref[pl.ds(c, half, stride=chans), :] = signal[:, c * BLOCK : (c + 1) * BLOCK]


def gate_kernel(key_hbm, value_hbm, grad_hbm, query_hbm, out_ref, held, sems):
    groups, both, _ = out_ref.shape
    pieces = sems.shape[1]
    rows = key_hbm.shape[0] // pieces
    part = groups // pieces

    def copy(i, p):
        span = pl.ds(p * rows, rows)
        source = (key_hbm, value_hbm, grad_hbm, query_hbm)[i]
        return pltpu.make_async_copy(source.at[span, :], held.at[i, span, :], sems.at[i, p])

    for p in range(pieces):
        for i in range(4):
            copy(i, p).start()
    for p in range(pieces):
        for i in range(4):
            copy(i, p).wait()
        span = pl.ds(p * rows, rows)
        key, value, grad, query = (held[i, span, :].astype(f32) for i in range(4))
        shape = (part, both // 2, BLOCK)
        kv, dz = (key * value).reshape(shape), (grad * query).reshape(shape)
        to = (p * part ^ FAR_IN) // part * part
        out_ref[pl.ds(to, part)] = swap_slots(jnp.concatenate([kv, dz], 1).astype(bf16), FAR_IN)


def filter_kernel(filter_ref, forward_ref, turn_ref, middle_ref, spec_ref, rows):
    chans, seq = filter_ref.shape
    half = seq // BLOCK
    for a, slot in enumerate(slots(half, FAR_IN)):
        rows[pl.ds(slot * chans, chans), :] = filter_ref[:, a * BLOCK : (a + 1) * BLOCK]
    spec_ref[...] = forward_rows(rows, chans, half, False, forward_ref, turn_ref, middle_ref)


def forward_kernel(both_ref, forward_ref, turn_ref, middle_ref, spec_ref, rows):
    half, both, _ = both_ref.shape
    rows[...] = both_ref[...].astype(f32).reshape(half * both, BLOCK)
    spec_ref[...] = forward_rows(rows, both, half, True, forward_ref, turn_ref, middle_ref)


def cross_kernel(spec_ref, back_ref, turn_ref, middle_ref, keep_ref, send_ref, out_rows):
    pairs, cores, own, chans, _ = keep_ref.shape
    half = 2 * pairs * cores * own
    count = chans * half
    kv_re, kv_im = spec_ref[:count, :BLOCK], spec_ref[:count, BLOCK:]
    dz_re, dz_im = spec_ref[count:, :BLOCK], spec_ref[count:, BLOCK:]
    cross = jnp.concatenate([kv_re * dz_re + kv_im * dz_im, kv_im * dz_re - kv_re * dz_im], 1)
    inverse_rows(cross, chans, half, out_rows, back_ref, turn_ref, middle_ref)
    bit = lax.rem(lax.div(lax.axis_index("dp"), 2), 2)
    size = out_rows.shape[0] // 4
    shape = keep_ref.shape[1:]
    for i in range(2):
        kept = pl.multiple_of((2 * i + bit) * size, size)
        sent = pl.multiple_of((2 * i + 1 - bit) * size, size)
        keep_ref[i] = out_rows[pl.ds(kept, size), :].reshape(shape)
        send_ref[i] = out_rows[pl.ds(sent, size), :].reshape(shape).astype(bf16)


def core_kernel(keep_ref, other_ref, mine_ref, send_ref):
    core = lax.rem(lax.axis_index("dp"), 2)
    for i in range(2):
        mine_ref[i] = keep_ref[i, core] + other_ref[i, core].astype(f32)
        send_ref[i] = (keep_ref[i, 1 - core] + other_ref[i, 1 - core].astype(f32)).astype(bf16)


def halve_kernel(keep_ref, other_ref, mine_ref, send_ref):
    place = lax.axis_index("dp")
    core, bit = lax.rem(place, 2), lax.div(place, 4)
    mine_ref[...] = keep_ref[bit] + other_ref[1 - core, bit].astype(f32)
    send_ref[...] = (keep_ref[1 - bit] + other_ref[1 - core, 1 - bit].astype(f32)).astype(bf16)


def conv_kernel(spec_ref, filter_ref, back_ref, turn_ref, middle_ref, after_ref, out_ref, out_rows):
    half, both, _ = out_ref.shape
    count = half * both // 2
    f_re, f_im = filter_ref[:, :BLOCK], filter_ref[:, BLOCK:]
    kv_re, kv_im = spec_ref[:count, :BLOCK], spec_ref[:count, BLOCK:]
    dz_re, dz_im = spec_ref[count:, :BLOCK], spec_ref[count:, BLOCK:]
    conv = jnp.concatenate([f_re * kv_re - f_im * kv_im, -f_re * kv_im - f_im * kv_re], 1)
    dkv = jnp.concatenate([f_re * dz_re + f_im * dz_im, f_im * dz_re - f_re * dz_im], 1)
    inverse_rows(
        jnp.concatenate([conv, dkv], 0), both, half, out_rows, back_ref, turn_ref, middle_ref
    )
    out_ref[...] = out_rows[...].reshape(half, both, BLOCK).astype(bf16)


def final_kernel(
    both_ref,
    key_ref,
    value_ref,
    grad_ref,
    keep_ref,
    other_ref,
    gq_ref,
    gk_ref,
    gv_ref,
    gf_ref,
    *,
    scale,
):
    lags = (keep_ref[...] + other_ref[...].astype(f32)) * scale
    for a in range(lags.shape[0]):
        gf_ref[:, a * BLOCK : (a + 1) * BLOCK] = lags[a]
    groups, both, _ = both_ref.shape
    chans = both // 2
    wide = swap_slots(both_ref[...], FAR_OUT).astype(f32)
    conv = wide[:, :chans, :].reshape(groups * chans, BLOCK)
    dkv = wide[:, chans:, :].reshape(groups * chans, BLOCK)
    gq_ref[...] = (grad_ref[...].astype(f32) * conv).astype(bf16)
    gk_ref[...] = (dkv * value_ref[...].astype(f32)).astype(bf16)
    gv_ref[...] = (dkv * key_ref[...].astype(f32)).astype(bf16)


def call(kernel, out, *args, scratch=(), flops=0, any_space=0, name=None):
    nbytes = sum(math.prod(a.shape) * a.dtype.itemsize for a in args)
    vmem = pl.BlockSpec(memory_space=pltpu.VMEM)
    return pl.pallas_call(
        kernel,
        out_shape=out,
        in_specs=[vmem] * (len(args) - any_space)
        + [pl.BlockSpec(memory_space=pl.ANY)] * any_space,
        out_specs=jax.tree.map(lambda _: vmem, out),
        scratch_shapes=[pltpu.VMEM(shape, f32) for shape in scratch],
        compiler_params=pltpu.CompilerParams(vmem_limit_bytes=40 * 2**20),
        cost_estimate=pl.CostEstimate(flops=flops, bytes_accessed=nbytes, transcendentals=0),
        name=name,
    )(*args)


def local(query_gate, key_gate, value_gate, grad_out, long_filter):
    chans, seq = long_filter.shape
    half = seq // BLOCK
    groups = lax.axis_size("dp")
    total = query_gate.shape[1]
    both = 2 * chans
    tables = {name: jnp.asarray(table) for name, table in make_tables(half, seq).items()}
    forward, back = tables["forward"], tables["back"]
    turn, middle, lag_back = tables["turn"], tables["middle"], tables["lag"]
    query, key, value, grad = (
        x.reshape(total, BLOCK) for x in (query_gate, key_gate, value_gate, grad_out)
    )
    shape = jax.ShapeDtypeStruct
    pieces = shape((half, both, BLOCK), bf16)
    work = 2 * chans * half * 256 * 768

    gated = pl.pallas_call(
        gate_kernel,
        out_shape=pieces,
        in_specs=[pl.BlockSpec(memory_space=pltpu.HBM)] * 4,
        out_specs=pl.BlockSpec(memory_space=pltpu.VMEM),
        scratch_shapes=[
            pltpu.VMEM((4, total, BLOCK), bf16),
            pltpu.SemaphoreType.DMA((4, 4)),
        ],
        compiler_params=pltpu.CompilerParams(vmem_limit_bytes=63 * 2**20),
        cost_estimate=pl.CostEstimate(
            flops=total * BLOCK * 2, bytes_accessed=total * BLOCK * 12, transcendentals=0
        ),
        name="gate",
    )(key, value, grad, query)
    here = lax.all_to_all(
        gated, "ctx", 0, 0, tiled=True, axis_index_groups=[slots(half, FAR_IN)]
    )
    filter_spec = call(
        filter_kernel,
        shape((chans * half, 2 * BLOCK), f32),
        long_filter,
        forward,
        turn,
        middle,
        scratch=[(half * chans, BLOCK)],
        flops=2 * work,
        name="filter",
    )
    spec = call(
        forward_kernel,
        shape((both * half, 2 * BLOCK), f32),
        here,
        forward,
        turn,
        middle,
        scratch=[(half * both, BLOCK)],
        flops=3 * work,
        name="forward",
    )
    own = half // groups
    quads = groups // 2
    quad = (own, chans, BLOCK)
    keep, send = call(
        cross_kernel,
        (shape((2, 2, *quad), f32), shape((2, 2, *quad), bf16)),
        spec,
        lag_back,
        turn,
        middle,
        scratch=[(half * chans, BLOCK)],
        flops=2 * work,
        name="cross",
    )
    other = lax.ppermute(send, "dp", [(i, i ^ 2) for i in range(groups)])
    carried = call(
        conv_kernel,
        pieces,
        spec,
        filter_spec,
        back,
        turn,
        middle,
        send,
        scratch=[(half * both, BLOCK)],
        flops=4 * work,
        any_space=1,
        name="conv",
    )
    keep, send = call(
        core_kernel,
        (shape((2, *quad), f32), shape((2, *quad), bf16)),
        keep,
        other,
        flops=HINT,
        name="core",
    )
    cores = [[2 * z, 2 * z + 1] for z in range(quads)]
    other = lax.all_gather(send, "dp", axis=0, axis_index_groups=cores)
    keep, send = call(
        halve_kernel,
        (shape(quad, f32), shape(quad, bf16)),
        keep,
        other,
        name="halve",
    )
    other = lax.ppermute(send, "dp", [(i, i ^ 4) for i in range(groups)])
    back_here = lax.all_to_all(
        carried, "ctx", 0, 0, tiled=True, axis_index_groups=[slots(half, FAR_OUT)]
    )
    *grads, grad_filter = call(
        functools.partial(final_kernel, scale=1.0 / math.sqrt(seq * groups)),
        (shape((total, BLOCK), bf16),) * 3 + (shape((chans, own * BLOCK), f32),),
        back_here,
        key,
        value,
        grad,
        keep,
        other,
        name="final",
    )
    return tuple(g[None] for g in grads) + (grad_filter,)


def solution(mesh):
    in_specs = (
        P("dp", None, "ctx"),
        P("dp", None, "ctx"),
        P("dp", None, "ctx"),
        P("dp", None, "ctx"),
        P("ctx", None),
    )
    out_specs = (P("dp", None, "ctx"), P("dp", None, "ctx"), P("dp", None, "ctx"), P("ctx", "dp"))
    return jax.shard_map(local, mesh=mesh, in_specs=in_specs, out_specs=out_specs, check_vma=False)
```

```python
import functools
import math

import jax
import jax.numpy as jnp
import numpy as np
from jax import lax
from jax.experimental import pallas as pl
from jax.experimental.pallas import tpu as pltpu
from jax.sharding import PartitionSpec as P

BLOCK = 128
bf16 = jnp.bfloat16
f32 = jnp.float32


FAR_IN, FAR_OUT = 58, 58
HINT = 30 * 10**9


def slots(count, far):
    return [m ^ far for m in range(count)]


def swap_slots(blocks, far):
    rest = blocks.shape[1:]
    for bit in (1 << b for b in range(6)):
        if far & bit and bit < blocks.shape[0]:
            pairs = blocks.reshape(blocks.shape[0] // (2 * bit), 2, bit, *rest)
            blocks = jnp.concatenate([pairs[:, 1:], pairs[:, :1]], 1).reshape(-1, *rest)
    return blocks


def split_table(table):
    high = table.astype(bf16)
    return high, (table - high.astype(np.float64)).astype(bf16)


def make_tables(half, seq):
    length = 2 * seq
    k = np.arange(half) + 0.5
    first = 2.0 * math.pi * np.outer(k, np.arange(half)) / (2 * half)
    turn = 2.0 * math.pi * np.outer(k, np.arange(BLOCK)) / length
    block = 2.0 * math.pi * np.outer(np.arange(BLOCK), np.arange(BLOCK)) / BLOCK
    came = slots(half, FAR_IN)
    first_high, first_low = split_table(np.concatenate([np.cos(first), -np.sin(first)], 0)[:, came])
    back = np.concatenate([np.cos(first).T, -np.sin(first).T], 1) * (2.0 / length)
    back = back.astype(bf16)
    cos, sin = np.cos(block), np.sin(block)
    mid_high, mid_low = split_table(np.block([[cos, -sin], [sin, cos]]))
    return {
        "forward": np.concatenate([first_high, first_high, first_low], 1),
        "back": back[slots(half, FAR_OUT)],
        "lag": back,
        "middle": np.concatenate([mid_high, mid_high, mid_low], 0),
        "turn": np.stack([np.cos(turn), np.sin(turn)]).astype(np.float32),
    }


def split(value):
    high = value.astype(bf16)
    return high, (value - high.astype(f32)).astype(bf16)


def dot(left, right):
    return jnp.dot(left, right, preferred_element_type=f32)


def middle_exact(rows, middle_ref):
    high, low = split(rows)
    return dot(jnp.concatenate([high, low, high], 1), middle_ref[...])


def forward_rows(rows_ref, chans, half, exact, forward_ref, turn_ref, middle_ref):
    cols = jnp.concatenate([rows_ref[pl.ds(c, half, stride=chans), :] for c in range(chans)], 1)
    if exact:
        high = cols.astype(bf16)
        table = jnp.concatenate([forward_ref[:, :half], forward_ref[:, 2 * half :]], 1)
        section = dot(table, jnp.concatenate([high, high], 0))
    else:
        high, low = split(cols)
        section = dot(forward_ref[...], jnp.concatenate([high, low, high], 0))
    cos, sin = turn_ref[0], turn_ref[1]
    rows = []
    for c in range(chans):
        re = section[:half, c * BLOCK : (c + 1) * BLOCK]
        im = section[half:, c * BLOCK : (c + 1) * BLOCK]
        rows.append(jnp.concatenate([re * cos + im * sin, im * cos - re * sin], 1))
    return middle_exact(jnp.concatenate(rows, 0), middle_ref)


def inverse_rows(spec, chans, half, out_ref, back_ref, turn_ref, middle_ref):
    inner = dot(spec.astype(bf16), middle_ref[: 2 * BLOCK, :])
    cos, sin = turn_ref[0], turn_ref[1]
    cols = []
    for c in range(chans):
        re = inner[c * half : (c + 1) * half, :BLOCK]
        minus = inner[c * half : (c + 1) * half, BLOCK:]
        cols.append(jnp.concatenate([re * cos + minus * sin, re * sin - minus * cos], 0))
    signal = dot(back_ref[...], jnp.concatenate(cols, 1).astype(bf16))
    for c in range(chans):
        out_ref[pl.ds(c, half, stride=chans), :] = signal[:, c * BLOCK : (c + 1) * BLOCK]


def gate_kernel(key_hbm, value_hbm, grad_hbm, query_hbm, out_ref, held, sems):
    groups, both, _ = out_ref.shape
    pieces = sems.shape[1]
    rows = key_hbm.shape[0] // pieces
    part = groups // pieces

    def copy(i, p):
        span = pl.ds(p * rows, rows)
        source = (key_hbm, value_hbm, grad_hbm, query_hbm)[i]
        return pltpu.make_async_copy(source.at[span, :], held.at[i, span, :], sems.at[i, p])

    for p in range(pieces):
        for i in range(4):
            copy(i, p).start()
    for p in range(pieces):
        for i in range(4):
            copy(i, p).wait()
        span = pl.ds(p * rows, rows)
        key, value, grad, query = (held[i, span, :].astype(f32) for i in range(4))
        shape = (part, both // 2, BLOCK)
        kv, dz = (key * value).reshape(shape), (grad * query).reshape(shape)
        to = (p * part ^ FAR_IN) // part * part
        out_ref[pl.ds(to, part)] = swap_slots(jnp.concatenate([kv, dz], 1).astype(bf16), FAR_IN)


def filter_kernel(filter_ref, forward_ref, turn_ref, middle_ref, spec_ref, rows):
    chans, seq = filter_ref.shape
    half = seq // BLOCK
    for a, slot in enumerate(slots(half, FAR_IN)):
        rows[pl.ds(slot * chans, chans), :] = filter_ref[:, a * BLOCK : (a + 1) * BLOCK]
    spec_ref[...] = forward_rows(rows, chans, half, False, forward_ref, turn_ref, middle_ref)


def forward_kernel(both_ref, forward_ref, turn_ref, middle_ref, spec_ref, rows):
    half, both, _ = both_ref.shape
    rows[...] = both_ref[...].astype(f32).reshape(half * both, BLOCK)
    spec_ref[...] = forward_rows(rows, both, half, True, forward_ref, turn_ref, middle_ref)


def cross_kernel(spec_ref, back_ref, turn_ref, middle_ref, keep_ref, send_ref, out_rows):
    pairs, cores, own, chans, _ = keep_ref.shape
    half = 2 * pairs * cores * own
    count = chans * half
    kv_re, kv_im = spec_ref[:count, :BLOCK], spec_ref[:count, BLOCK:]
    dz_re, dz_im = spec_ref[count:, :BLOCK], spec_ref[count:, BLOCK:]
    cross = jnp.concatenate([kv_re * dz_re + kv_im * dz_im, kv_im * dz_re - kv_re * dz_im], 1)
    inverse_rows(cross, chans, half, out_rows, back_ref, turn_ref, middle_ref)
    bit = lax.rem(lax.div(lax.axis_index("dp"), 2), 2)
    size = out_rows.shape[0] // 4
    shape = keep_ref.shape[1:]
    for i in range(2):
        kept = pl.multiple_of((2 * i + bit) * size, size)
        sent = pl.multiple_of((2 * i + 1 - bit) * size, size)
        keep_ref[i] = out_rows[pl.ds(kept, size), :].reshape(shape)
        send_ref[i] = out_rows[pl.ds(sent, size), :].reshape(shape).astype(bf16)


def core_kernel(keep_ref, other_ref, mine_ref, send_ref):
    core = lax.rem(lax.axis_index("dp"), 2)
    for i in range(2):
        mine_ref[i] = keep_ref[i, core] + other_ref[i, core].astype(f32)
        send_ref[i] = (keep_ref[i, 1 - core] + other_ref[i, 1 - core].astype(f32)).astype(bf16)


def halve_kernel(keep_ref, other_ref, mine_ref, send_ref):
    place = lax.axis_index("dp")
    core, bit = lax.rem(place, 2), lax.div(place, 4)
    mine_ref[...] = keep_ref[bit] + other_ref[1 - core, bit].astype(f32)
    send_ref[...] = (keep_ref[1 - bit] + other_ref[1 - core, 1 - bit].astype(f32)).astype(bf16)


def conv_kernel(spec_ref, filter_ref, back_ref, turn_ref, middle_ref, after_ref, out_ref, out_rows):
    half, both, _ = out_ref.shape
    count = half * both // 2
    f_re, f_im = filter_ref[:, :BLOCK], filter_ref[:, BLOCK:]
    kv_re, kv_im = spec_ref[:count, :BLOCK], spec_ref[:count, BLOCK:]
    dz_re, dz_im = spec_ref[count:, :BLOCK], spec_ref[count:, BLOCK:]
    conv = jnp.concatenate([f_re * kv_re - f_im * kv_im, -f_re * kv_im - f_im * kv_re], 1)
    dkv = jnp.concatenate([f_re * dz_re + f_im * dz_im, f_im * dz_re - f_re * dz_im], 1)
    inverse_rows(
        jnp.concatenate([conv, dkv], 0), both, half, out_rows, back_ref, turn_ref, middle_ref
    )
    out_ref[...] = out_rows[...].reshape(half, both, BLOCK).astype(bf16)


def final_kernel(
    both_ref,
    key_ref,
    value_ref,
    grad_ref,
    keep_ref,
    other_ref,
    gq_ref,
    gk_ref,
    gv_ref,
    gf_ref,
    *,
    scale,
):
    side = lax.div(lax.axis_index("dp"), 4)
    lags = (keep_ref[...] + other_ref[1 - side].astype(f32)) * scale
    for a in range(lags.shape[0]):
        gf_ref[:, a * BLOCK : (a + 1) * BLOCK] = lags[a]
    groups, both, _ = both_ref.shape
    chans = both // 2
    wide = swap_slots(both_ref[...], FAR_OUT).astype(f32)
    conv = wide[:, :chans, :].reshape(groups * chans, BLOCK)
    dkv = wide[:, chans:, :].reshape(groups * chans, BLOCK)
    gq_ref[...] = (grad_ref[...].astype(f32) * conv).astype(bf16)
    gk_ref[...] = (dkv * value_ref[...].astype(f32)).astype(bf16)
    gv_ref[...] = (dkv * key_ref[...].astype(f32)).astype(bf16)


def call(kernel, out, *args, scratch=(), flops=0, any_space=0, name=None):
    nbytes = sum(math.prod(a.shape) * a.dtype.itemsize for a in args)
    vmem = pl.BlockSpec(memory_space=pltpu.VMEM)
    return pl.pallas_call(
        kernel,
        out_shape=out,
        in_specs=[vmem] * (len(args) - any_space)
        + [pl.BlockSpec(memory_space=pl.ANY)] * any_space,
        out_specs=jax.tree.map(lambda _: vmem, out),
        scratch_shapes=[pltpu.VMEM(shape, f32) for shape in scratch],
        compiler_params=pltpu.CompilerParams(vmem_limit_bytes=40 * 2**20),
        cost_estimate=pl.CostEstimate(flops=flops, bytes_accessed=nbytes, transcendentals=0),
        name=name,
    )(*args)


def local(query_gate, key_gate, value_gate, grad_out, long_filter):
    chans, seq = long_filter.shape
    half = seq // BLOCK
    groups = lax.axis_size("dp")
    total = query_gate.shape[1]
    both = 2 * chans
    tables = {name: jnp.asarray(table) for name, table in make_tables(half, seq).items()}
    forward, back = tables["forward"], tables["back"]
    turn, middle, lag_back = tables["turn"], tables["middle"], tables["lag"]
    query, key, value, grad = (
        x.reshape(total, BLOCK) for x in (query_gate, key_gate, value_gate, grad_out)
    )
    shape = jax.ShapeDtypeStruct
    pieces = shape((half, both, BLOCK), bf16)
    work = 2 * chans * half * 256 * 768

    gated = pl.pallas_call(
        gate_kernel,
        out_shape=pieces,
        in_specs=[pl.BlockSpec(memory_space=pltpu.HBM)] * 4,
        out_specs=pl.BlockSpec(memory_space=pltpu.VMEM),
        scratch_shapes=[
            pltpu.VMEM((4, total, BLOCK), bf16),
            pltpu.SemaphoreType.DMA((4, 4)),
        ],
        compiler_params=pltpu.CompilerParams(vmem_limit_bytes=63 * 2**20),
        cost_estimate=pl.CostEstimate(
            flops=total * BLOCK * 2, bytes_accessed=total * BLOCK * 12, transcendentals=0
        ),
        name="gate",
    )(key, value, grad, query)
    here = lax.all_to_all(
        gated, "ctx", 0, 0, tiled=True, axis_index_groups=[slots(half, FAR_IN)]
    )
    filter_spec = call(
        filter_kernel,
        shape((chans * half, 2 * BLOCK), f32),
        long_filter,
        forward,
        turn,
        middle,
        scratch=[(half * chans, BLOCK)],
        flops=2 * work,
        name="filter",
    )
    spec = call(
        forward_kernel,
        shape((both * half, 2 * BLOCK), f32),
        here,
        forward,
        turn,
        middle,
        scratch=[(half * both, BLOCK)],
        flops=3 * work,
        name="forward",
    )
    own = half // groups
    quads = groups // 2
    quad = (own, chans, BLOCK)
    keep, send = call(
        cross_kernel,
        (shape((2, 2, *quad), f32), shape((2, 2, *quad), bf16)),
        spec,
        lag_back,
        turn,
        middle,
        scratch=[(half * chans, BLOCK)],
        flops=2 * work,
        name="cross",
    )
    other = lax.ppermute(send, "dp", [(i, i ^ 2) for i in range(groups)])
    carried = call(
        conv_kernel,
        pieces,
        spec,
        filter_spec,
        back,
        turn,
        middle,
        send,
        scratch=[(half * both, BLOCK)],
        flops=4 * work,
        any_space=1,
        name="conv",
    )
    keep, send = call(
        core_kernel,
        (shape((2, *quad), f32), shape((2, *quad), bf16)),
        keep,
        other,
        flops=HINT,
        name="core",
    )
    cores = [[2 * z, 2 * z + 1] for z in range(quads)]
    other = lax.all_gather(send, "dp", axis=0, axis_index_groups=cores)
    keep, send = call(
        halve_kernel,
        (shape(quad, f32), shape(quad, bf16)),
        keep,
        other,
        name="halve",
    )
    sides = [[i, i + 4] for i in range(groups // 2)]
    other = lax.all_gather(send, "dp", axis=0, axis_index_groups=sides)
    back_here = lax.all_to_all(
        carried, "ctx", 0, 0, tiled=True, axis_index_groups=[slots(half, FAR_OUT)]
    )
    *grads, grad_filter = call(
        functools.partial(final_kernel, scale=1.0 / math.sqrt(seq * groups)),
        (shape((total, BLOCK), bf16),) * 3 + (shape((chans, own * BLOCK), f32),),
        back_here,
        key,
        value,
        grad,
        keep,
        other,
        name="final",
    )
    return tuple(g[None] for g in grads) + (grad_filter,)


def solution(mesh):
    in_specs = (
        P("dp", None, "ctx"),
        P("dp", None, "ctx"),
        P("dp", None, "ctx"),
        P("dp", None, "ctx"),
        P("ctx", None),
    )
    out_specs = (P("dp", None, "ctx"), P("dp", None, "ctx"), P("dp", None, "ctx"), P("ctx", "dp"))
    return jax.shard_map(local, mesh=mesh, in_specs=in_specs, out_specs=out_specs, check_vma=False)
```

```python
import functools
import math

import jax
import jax.numpy as jnp
import numpy as np
from jax import lax
from jax.experimental import pallas as pl
from jax.experimental.pallas import tpu as pltpu
from jax.sharding import PartitionSpec as P

BLOCK = 128
bf16 = jnp.bfloat16
f32 = jnp.float32


FAR_IN, FAR_OUT = 58, 58
HINT = 30 * 10**9


def slots(count, far):
    return [m ^ far for m in range(count)]


def swap_slots(blocks, far):
    rest = blocks.shape[1:]
    for bit in (1 << b for b in range(6)):
        if far & bit and bit < blocks.shape[0]:
            pairs = blocks.reshape(blocks.shape[0] // (2 * bit), 2, bit, *rest)
            blocks = jnp.concatenate([pairs[:, 1:], pairs[:, :1]], 1).reshape(-1, *rest)
    return blocks


def split_table(table):
    high = table.astype(bf16)
    return high, (table - high.astype(np.float64)).astype(bf16)


def make_tables(half, seq):
    length = 2 * seq
    k = np.arange(half) + 0.5
    first = 2.0 * math.pi * np.outer(k, np.arange(half)) / (2 * half)
    turn = 2.0 * math.pi * np.outer(k, np.arange(BLOCK)) / length
    block = 2.0 * math.pi * np.outer(np.arange(BLOCK), np.arange(BLOCK)) / BLOCK
    came = slots(half, FAR_IN)
    first_high, first_low = split_table(np.concatenate([np.cos(first), -np.sin(first)], 0)[:, came])
    back = np.concatenate([np.cos(first).T, -np.sin(first).T], 1) * (2.0 / length)
    back = back.astype(bf16)
    cos, sin = np.cos(block), np.sin(block)
    mid_high, mid_low = split_table(np.block([[cos, -sin], [sin, cos]]))
    return {
        "forward": np.concatenate([first_high, first_high, first_low], 1),
        "back": back[slots(half, FAR_OUT)],
        "lag": back,
        "middle": np.concatenate([mid_high, mid_high, mid_low], 0),
        "turn": np.stack([np.cos(turn), np.sin(turn)]).astype(np.float32),
    }


def split(value):
    high = value.astype(bf16)
    return high, (value - high.astype(f32)).astype(bf16)


def dot(left, right):
    return jnp.dot(left, right, preferred_element_type=f32)


def middle_exact(rows, middle_ref):
    high, low = split(rows)
    return dot(jnp.concatenate([high, low, high], 1), middle_ref[...])


def forward_rows(rows_ref, chans, half, exact, forward_ref, turn_ref, middle_ref):
    cols = jnp.concatenate([rows_ref[pl.ds(c, half, stride=chans), :] for c in range(chans)], 1)
    if exact:
        high = cols.astype(bf16)
        table = jnp.concatenate([forward_ref[:, :half], forward_ref[:, 2 * half :]], 1)
        section = dot(table, jnp.concatenate([high, high], 0))
    else:
        high, low = split(cols)
        section = dot(forward_ref[...], jnp.concatenate([high, low, high], 0))
    cos, sin = turn_ref[0], turn_ref[1]
    rows = []
    for c in range(chans):
        re = section[:half, c * BLOCK : (c + 1) * BLOCK]
        im = section[half:, c * BLOCK : (c + 1) * BLOCK]
        rows.append(jnp.concatenate([re * cos + im * sin, im * cos - re * sin], 1))
    rows = jnp.concatenate(rows, 0)
    if exact:
        return dot(rows.astype(bf16), middle_ref[: 2 * BLOCK, :])
    return middle_exact(rows, middle_ref)


def inverse_rows(spec, chans, half, out_ref, back_ref, turn_ref, middle_ref):
    inner = dot(spec.astype(bf16), middle_ref[: 2 * BLOCK, :])
    cos, sin = turn_ref[0], turn_ref[1]
    cols = []
    for c in range(chans):
        re = inner[c * half : (c + 1) * half, :BLOCK]
        minus = inner[c * half : (c + 1) * half, BLOCK:]
        cols.append(jnp.concatenate([re * cos + minus * sin, re * sin - minus * cos], 0))
    signal = dot(back_ref[...], jnp.concatenate(cols, 1).astype(bf16))
    for c in range(chans):
        out_ref[pl.ds(c, half, stride=chans), :] = signal[:, c * BLOCK : (c + 1) * BLOCK]


def gate_kernel(key_hbm, value_hbm, grad_hbm, query_hbm, out_ref, held, sems):
    groups, both, _ = out_ref.shape
    pieces = sems.shape[1]
    rows = key_hbm.shape[0] // pieces
    part = groups // pieces

    def copy(i, p):
        span = pl.ds(p * rows, rows)
        source = (key_hbm, value_hbm, grad_hbm, query_hbm)[i]
        return pltpu.make_async_copy(source.at[span, :], held.at[i, span, :], sems.at[i, p])

    for p in range(pieces):
        for i in range(4):
            copy(i, p).start()
    for p in range(pieces):
        for i in range(4):
            copy(i, p).wait()
        span = pl.ds(p * rows, rows)
        key, value, grad, query = (held[i, span, :].astype(f32) for i in range(4))
        shape = (part, both // 2, BLOCK)
        kv, dz = (key * value).reshape(shape), (grad * query).reshape(shape)
        to = (p * part ^ FAR_IN) // part * part
        out_ref[pl.ds(to, part)] = swap_slots(jnp.concatenate([kv, dz], 1).astype(bf16), FAR_IN)


def filter_kernel(filter_ref, forward_ref, turn_ref, middle_ref, spec_ref, rows):
    chans, seq = filter_ref.shape
    half = seq // BLOCK
    for a, slot in enumerate(slots(half, FAR_IN)):
        rows[pl.ds(slot * chans, chans), :] = filter_ref[:, a * BLOCK : (a + 1) * BLOCK]
    spec_ref[...] = forward_rows(rows, chans, half, False, forward_ref, turn_ref, middle_ref)


def cross_terms(spec_ref, back_ref, turn_ref, middle_ref, keep_ref, send_ref, out_rows):
    pairs, cores, own, chans, _ = keep_ref.shape
    half = 2 * pairs * cores * own
    count = chans * half
    kv_re, kv_im = spec_ref[:count, :BLOCK], spec_ref[:count, BLOCK:]
    dz_re, dz_im = spec_ref[count:, :BLOCK], spec_ref[count:, BLOCK:]
    cross = jnp.concatenate([kv_re * dz_re + kv_im * dz_im, kv_im * dz_re - kv_re * dz_im], 1)
    inverse_rows(cross, chans, half, out_rows, back_ref, turn_ref, middle_ref)
    bit = lax.rem(lax.div(lax.axis_index("dp"), 2), 2)
    size = out_rows.shape[0] // 4
    shape = keep_ref.shape[1:]
    for i in range(2):
        kept = pl.multiple_of((2 * i + bit) * size, size)
        sent = pl.multiple_of((2 * i + 1 - bit) * size, size)
        keep_ref[i] = out_rows[pl.ds(kept, size), :].reshape(shape)
        send_ref[i] = out_rows[pl.ds(sent, size), :].reshape(shape).astype(bf16)


def core_kernel(keep_ref, other_ref, mine_ref, send_ref):
    core = lax.rem(lax.axis_index("dp"), 2)
    for i in range(2):
        mine_ref[i] = keep_ref[i, core] + other_ref[i, core].astype(f32)
        send_ref[i] = (keep_ref[i, 1 - core] + other_ref[i, 1 - core].astype(f32)).astype(bf16)


def halve_kernel(keep_ref, other_ref, mine_ref, send_ref):
    place = lax.axis_index("dp")
    core, bit = lax.rem(place, 2), lax.div(place, 4)
    mine_ref[...] = keep_ref[bit] + other_ref[1 - core, bit].astype(f32)
    send_ref[...] = (keep_ref[1 - bit] + other_ref[1 - core, 1 - bit].astype(f32)).astype(bf16)


def transform_kernel(
    both_ref,
    filter_ref,
    forward_ref,
    back_ref,
    lag_ref,
    turn_ref,
    middle_ref,
    out_hbm,
    keep_ref,
    send_ref,
    spec_ref,
    out_rows,
    lag_rows,
    made,
    sem,
):
    half, both, _ = out_hbm.shape
    out_rows[...] = both_ref[...].astype(f32).reshape(half * both, BLOCK)
    spec_ref[...] = forward_rows(out_rows, both, half, True, forward_ref, turn_ref, middle_ref)
    count = half * both // 2
    f_re, f_im = filter_ref[:, :BLOCK], filter_ref[:, BLOCK:]
    kv_re, kv_im = spec_ref[:count, :BLOCK], spec_ref[:count, BLOCK:]
    dz_re, dz_im = spec_ref[count:, :BLOCK], spec_ref[count:, BLOCK:]
    conv = jnp.concatenate([f_re * kv_re - f_im * kv_im, -f_re * kv_im - f_im * kv_re], 1)
    dkv = jnp.concatenate([f_re * dz_re + f_im * dz_im, f_im * dz_re - f_re * dz_im], 1)
    inverse_rows(
        jnp.concatenate([conv, dkv], 0), both, half, out_rows, back_ref, turn_ref, middle_ref
    )
    made[...] = out_rows[...].reshape(half, both, BLOCK).astype(bf16)
    done = pltpu.make_async_copy(made, out_hbm, sem)
    done.start()
    cross_terms(spec_ref, lag_ref, turn_ref, middle_ref, keep_ref, send_ref, lag_rows)
    done.wait()


def final_kernel(
    both_ref,
    key_ref,
    value_ref,
    grad_ref,
    keep_ref,
    other_ref,
    gq_ref,
    gk_ref,
    gv_ref,
    gf_ref,
    *,
    scale,
):
    side = lax.div(lax.axis_index("dp"), 4)
    lags = (keep_ref[...] + other_ref[1 - side].astype(f32)) * scale
    for a in range(lags.shape[0]):
        gf_ref[:, a * BLOCK : (a + 1) * BLOCK] = lags[a]
    groups, both, _ = both_ref.shape
    chans = both // 2
    wide = swap_slots(both_ref[...], FAR_OUT).astype(f32)
    conv = wide[:, :chans, :].reshape(groups * chans, BLOCK)
    dkv = wide[:, chans:, :].reshape(groups * chans, BLOCK)
    gq_ref[...] = (grad_ref[...].astype(f32) * conv).astype(bf16)
    gk_ref[...] = (dkv * value_ref[...].astype(f32)).astype(bf16)
    gv_ref[...] = (dkv * key_ref[...].astype(f32)).astype(bf16)


def call(kernel, out, *args, scratch=(), flops=0, any_space=0, name=None):
    nbytes = sum(math.prod(a.shape) * a.dtype.itemsize for a in args)
    vmem = pl.BlockSpec(memory_space=pltpu.VMEM)
    return pl.pallas_call(
        kernel,
        out_shape=out,
        in_specs=[vmem] * (len(args) - any_space)
        + [pl.BlockSpec(memory_space=pl.ANY)] * any_space,
        out_specs=jax.tree.map(lambda _: vmem, out),
        scratch_shapes=[pltpu.VMEM(shape, f32) for shape in scratch],
        compiler_params=pltpu.CompilerParams(vmem_limit_bytes=40 * 2**20),
        cost_estimate=pl.CostEstimate(flops=flops, bytes_accessed=nbytes, transcendentals=0),
        name=name,
    )(*args)


def local(query_gate, key_gate, value_gate, grad_out, long_filter):
    chans, seq = long_filter.shape
    half = seq // BLOCK
    groups = lax.axis_size("dp")
    total = query_gate.shape[1]
    both = 2 * chans
    tables = {name: jnp.asarray(table) for name, table in make_tables(half, seq).items()}
    forward, back = tables["forward"], tables["back"]
    turn, middle, lag_back = tables["turn"], tables["middle"], tables["lag"]
    query, key, value, grad = (
        x.reshape(total, BLOCK) for x in (query_gate, key_gate, value_gate, grad_out)
    )
    shape = jax.ShapeDtypeStruct
    pieces = shape((half, both, BLOCK), bf16)
    work = 2 * chans * half * 256 * 768

    gated = pl.pallas_call(
        gate_kernel,
        out_shape=pieces,
        in_specs=[pl.BlockSpec(memory_space=pltpu.HBM)] * 4,
        out_specs=pl.BlockSpec(memory_space=pltpu.VMEM),
        scratch_shapes=[
            pltpu.VMEM((4, total, BLOCK), bf16),
            pltpu.SemaphoreType.DMA((4, 4)),
        ],
        compiler_params=pltpu.CompilerParams(vmem_limit_bytes=63 * 2**20),
        cost_estimate=pl.CostEstimate(
            flops=total * BLOCK * 2, bytes_accessed=total * BLOCK * 12, transcendentals=0
        ),
        name="gate",
    )(key, value, grad, query)
    here = lax.all_to_all(
        gated, "ctx", 0, 0, tiled=True, axis_index_groups=[slots(half, FAR_IN)]
    )
    filter_spec = call(
        filter_kernel,
        shape((chans * half, 2 * BLOCK), f32),
        long_filter,
        forward,
        turn,
        middle,
        scratch=[(half * chans, BLOCK)],
        flops=2 * work,
        name="filter",
    )
    own = half // groups
    quads = groups // 2
    quad = (own, chans, BLOCK)
    vmem = pl.BlockSpec(memory_space=pltpu.VMEM)
    carried, keep, send = pl.pallas_call(
        transform_kernel,
        out_shape=(pieces, shape((2, 2, *quad), f32), shape((2, 2, *quad), bf16)),
        in_specs=[vmem] * 7,
        out_specs=(pl.BlockSpec(memory_space=pltpu.HBM), vmem, vmem),
        scratch_shapes=[
            pltpu.VMEM((both * half, 2 * BLOCK), f32),
            pltpu.VMEM((half * both, BLOCK), f32),
            pltpu.VMEM((half * chans, BLOCK), f32),
            pltpu.VMEM((half, both, BLOCK), bf16),
            pltpu.SemaphoreType.DMA(()),
        ],
        compiler_params=pltpu.CompilerParams(vmem_limit_bytes=40 * 2**20),
        cost_estimate=pl.CostEstimate(flops=6 * work, bytes_accessed=2**21, transcendentals=0),
        name="transform",
    )(here, filter_spec, forward, back, lag_back, turn, middle)
    other = lax.ppermute(send, "dp", [(i, i ^ 2) for i in range(groups)])
    keep, send = call(
        core_kernel,
        (shape((2, *quad), f32), shape((2, *quad), bf16)),
        keep,
        other,
        flops=HINT,
        name="core",
    )
    cores = [[2 * z, 2 * z + 1] for z in range(quads)]
    other = lax.all_gather(send, "dp", axis=0, axis_index_groups=cores)
    keep, send = call(
        halve_kernel,
        (shape(quad, f32), shape(quad, bf16)),
        keep,
        other,
        name="halve",
    )
    sides = [[i, i + 4] for i in range(groups // 2)]
    other = lax.all_gather(send, "dp", axis=0, axis_index_groups=sides)
    back_here = lax.all_to_all(
        carried, "ctx", 0, 0, tiled=True, axis_index_groups=[slots(half, FAR_OUT)]
    )
    *grads, grad_filter = call(
        functools.partial(final_kernel, scale=1.0 / math.sqrt(seq * groups)),
        (shape((total, BLOCK), bf16),) * 3 + (shape((chans, own * BLOCK), f32),),
        back_here,
        key,
        value,
        grad,
        keep,
        other,
        name="final",
    )
    return tuple(g[None] for g in grads) + (grad_filter,)


def solution(mesh):
    in_specs = (
        P("dp", None, "ctx"),
        P("dp", None, "ctx"),
        P("dp", None, "ctx"),
        P("dp", None, "ctx"),
        P("ctx", None),
    )
    out_specs = (P("dp", None, "ctx"), P("dp", None, "ctx"), P("dp", None, "ctx"), P("ctx", "dp"))
    return jax.shard_map(local, mesh=mesh, in_specs=in_specs, out_specs=out_specs, check_vma=False)
```

```python
import functools
import math

import jax
import jax.numpy as jnp
import numpy as np
from jax import lax
from jax.experimental import pallas as pl
from jax.experimental.pallas import tpu as pltpu
from jax.sharding import PartitionSpec as P

BLOCK = 128
bf16 = jnp.bfloat16
f32 = jnp.float32


FAR_IN, FAR_OUT = 58, 58
HINT = 30 * 10**9


def slots(count, far):
    return [m ^ far for m in range(count)]


def swap_slots(blocks, far):
    rest = blocks.shape[1:]
    for bit in (1 << b for b in range(6)):
        if far & bit and bit < blocks.shape[0]:
            pairs = blocks.reshape(blocks.shape[0] // (2 * bit), 2, bit, *rest)
            blocks = jnp.concatenate([pairs[:, 1:], pairs[:, :1]], 1).reshape(-1, *rest)
    return blocks


def split_table(table):
    high = table.astype(bf16)
    return high, (table - high.astype(np.float64)).astype(bf16)


def make_tables(half, seq):
    length = 2 * seq
    k = np.arange(half) + 0.5
    first = 2.0 * math.pi * np.outer(k, np.arange(half)) / (2 * half)
    turn = 2.0 * math.pi * np.outer(k, np.arange(BLOCK)) / length
    block = 2.0 * math.pi * np.outer(np.arange(BLOCK), np.arange(BLOCK)) / BLOCK
    came = slots(half, FAR_IN)
    first_high, first_low = split_table(np.concatenate([np.cos(first), -np.sin(first)], 0)[:, came])
    back = np.concatenate([np.cos(first).T, -np.sin(first).T], 1) * (2.0 / length)
    back = back.astype(bf16)
    cos, sin = np.cos(block), np.sin(block)
    mid_high, mid_low = split_table(np.block([[cos, -sin], [sin, cos]]))
    return {
        "forward": np.concatenate([first_high, first_high, first_low], 1),
        "exact": np.concatenate([first_high, first_low], 1),
        "back": back[slots(half, FAR_OUT)],
        "lag": back,
        "middle": np.concatenate([mid_high, mid_high, mid_low], 0),
        "turn": np.stack([np.cos(turn), np.sin(turn)]).astype(np.float32),
    }


def split(value):
    high = value.astype(bf16)
    return high, (value - high.astype(f32)).astype(bf16)


def dot(left, right):
    return jnp.dot(left, right, preferred_element_type=f32)


def middle_exact(rows, middle_ref):
    high, low = split(rows)
    return dot(jnp.concatenate([high, low, high], 1), middle_ref[...])


def forward_rows(rows_ref, chans, half, exact, forward_ref, turn_ref, middle_ref):
    cols = jnp.concatenate([rows_ref[pl.ds(c, half, stride=chans), :] for c in range(chans)], 1)
    if exact:
        high = cols.astype(bf16)
        section = dot(forward_ref[...], jnp.concatenate([high, high], 0))
    else:
        high, low = split(cols)
        section = dot(forward_ref[...], jnp.concatenate([high, low, high], 0))
    cos, sin = turn_ref[0], turn_ref[1]
    rows = []
    for c in range(chans):
        re = section[:half, c * BLOCK : (c + 1) * BLOCK]
        im = section[half:, c * BLOCK : (c + 1) * BLOCK]
        rows.append(jnp.concatenate([re * cos + im * sin, im * cos - re * sin], 1))
    rows = jnp.concatenate(rows, 0)
    if exact:
        return dot(rows.astype(bf16), middle_ref[: 2 * BLOCK, :])
    return middle_exact(rows, middle_ref)


def inverse_rows(spec, chans, half, out_ref, back_ref, turn_ref, middle_ref):
    inner = dot(spec.astype(bf16), middle_ref[: 2 * BLOCK, :])
    cos, sin = turn_ref[0], turn_ref[1]
    cols = []
    for c in range(chans):
        re = inner[c * half : (c + 1) * half, :BLOCK]
        minus = inner[c * half : (c + 1) * half, BLOCK:]
        cols.append(jnp.concatenate([re * cos + minus * sin, re * sin - minus * cos], 0))
    signal = dot(back_ref[...], jnp.concatenate(cols, 1).astype(bf16))
    for c in range(chans):
        out_ref[pl.ds(c, half, stride=chans), :] = signal[:, c * BLOCK : (c + 1) * BLOCK]


def gate_kernel(key_hbm, value_hbm, grad_hbm, query_hbm, out_ref, held, sems):
    groups, both, _ = out_ref.shape
    pieces = sems.shape[1]
    rows = key_hbm.shape[0] // pieces
    part = groups // pieces

    def copy(i, p):
        span = pl.ds(p * rows, rows)
        source = (key_hbm, value_hbm, grad_hbm, query_hbm)[i]
        return pltpu.make_async_copy(source.at[span, :], held.at[i, span, :], sems.at[i, p])

    for p in range(pieces):
        for i in range(4):
            copy(i, p).start()
    for p in range(pieces):
        for i in range(4):
            copy(i, p).wait()
        span = pl.ds(p * rows, rows)
        key, value, grad, query = (held[i, span, :].astype(f32) for i in range(4))
        shape = (part, both // 2, BLOCK)
        kv, dz = (key * value).reshape(shape), (grad * query).reshape(shape)
        to = (p * part ^ FAR_IN) // part * part
        out_ref[pl.ds(to, part)] = swap_slots(jnp.concatenate([kv, dz], 1).astype(bf16), FAR_IN)


def filter_kernel(filter_ref, forward_ref, turn_ref, middle_ref, spec_ref, rows):
    chans, seq = filter_ref.shape
    half = seq // BLOCK
    for a, slot in enumerate(slots(half, FAR_IN)):
        rows[pl.ds(slot * chans, chans), :] = filter_ref[:, a * BLOCK : (a + 1) * BLOCK]
    spec_ref[...] = forward_rows(rows, chans, half, False, forward_ref, turn_ref, middle_ref)


def cross_terms(spec_ref, back_ref, turn_ref, middle_ref, keep_ref, send_ref, out_rows):
    pairs, cores, own, chans, _ = keep_ref.shape
    half = 2 * pairs * cores * own
    count = chans * half
    kv_re, kv_im = spec_ref[:count, :BLOCK], spec_ref[:count, BLOCK:]
    dz_re, dz_im = spec_ref[count:, :BLOCK], spec_ref[count:, BLOCK:]
    cross = jnp.concatenate([kv_re * dz_re + kv_im * dz_im, kv_im * dz_re - kv_re * dz_im], 1)
    inverse_rows(cross, chans, half, out_rows, back_ref, turn_ref, middle_ref)
    bit = lax.rem(lax.div(lax.axis_index("dp"), 2), 2)
    size = out_rows.shape[0] // 4
    shape = keep_ref.shape[1:]
    for i in range(2):
        kept = pl.multiple_of((2 * i + bit) * size, size)
        sent = pl.multiple_of((2 * i + 1 - bit) * size, size)
        keep_ref[i] = out_rows[pl.ds(kept, size), :].reshape(shape)
        send_ref[i] = out_rows[pl.ds(sent, size), :].reshape(shape).astype(bf16)


def core_kernel(keep_ref, other_ref, mine_ref, send_ref):
    core = lax.rem(lax.axis_index("dp"), 2)
    for i in range(2):
        mine_ref[i] = keep_ref[i, core] + other_ref[i, core].astype(f32)
        send_ref[i] = (keep_ref[i, 1 - core] + other_ref[i, 1 - core].astype(f32)).astype(bf16)


def halve_kernel(keep_ref, other_ref, mine_ref, send_ref):
    place = lax.axis_index("dp")
    core, bit = lax.rem(place, 2), lax.div(place, 4)
    mine_ref[...] = keep_ref[bit] + other_ref[1 - core, bit].astype(f32)
    send_ref[...] = (keep_ref[1 - bit] + other_ref[1 - core, 1 - bit].astype(f32)).astype(bf16)


def transform_kernel(
    both_ref,
    filter_ref,
    forward_ref,
    back_ref,
    lag_ref,
    turn_ref,
    middle_ref,
    out_hbm,
    keep_ref,
    send_ref,
    spec_ref,
    out_rows,
    lag_rows,
    made,
    sem,
):
    half, both, _ = out_hbm.shape
    out_rows[...] = both_ref[...].astype(f32).reshape(half * both, BLOCK)
    spec_ref[...] = forward_rows(out_rows, both, half, True, forward_ref, turn_ref, middle_ref)
    count = half * both // 2
    f_re, f_im = filter_ref[:, :BLOCK], filter_ref[:, BLOCK:]
    kv_re, kv_im = spec_ref[:count, :BLOCK], spec_ref[:count, BLOCK:]
    dz_re, dz_im = spec_ref[count:, :BLOCK], spec_ref[count:, BLOCK:]
    conv = jnp.concatenate([f_re * kv_re - f_im * kv_im, -f_re * kv_im - f_im * kv_re], 1)
    dkv = jnp.concatenate([f_re * dz_re + f_im * dz_im, f_im * dz_re - f_re * dz_im], 1)
    inverse_rows(
        jnp.concatenate([conv, dkv], 0), both, half, out_rows, back_ref, turn_ref, middle_ref
    )
    sent = []
    part = half // 2
    for p in range(2):
        span = pl.ds(p * part, part)
        rows = out_rows[p * part * both : (p + 1) * part * both, :]
        made[span] = rows.reshape(part, both, BLOCK).astype(bf16)
        sent.append(pltpu.make_async_copy(made.at[span], out_hbm.at[span], sem.at[p]))
        sent[p].start()
    cross_terms(spec_ref, lag_ref, turn_ref, middle_ref, keep_ref, send_ref, lag_rows)
    for done in sent:
        done.wait()


def final_kernel(
    both_ref,
    key_ref,
    value_ref,
    grad_ref,
    keep_ref,
    other_ref,
    gq_ref,
    gk_ref,
    gv_ref,
    gf_ref,
    *,
    scale,
):
    side = lax.div(lax.axis_index("dp"), 4)
    lags = (keep_ref[...] + other_ref[1 - side].astype(f32)) * scale
    for a in range(lags.shape[0]):
        gf_ref[:, a * BLOCK : (a + 1) * BLOCK] = lags[a]
    groups, both, _ = both_ref.shape
    chans = both // 2
    wide = swap_slots(both_ref[...], FAR_OUT).astype(f32)
    conv = wide[:, :chans, :].reshape(groups * chans, BLOCK)
    dkv = wide[:, chans:, :].reshape(groups * chans, BLOCK)
    gq_ref[...] = (grad_ref[...].astype(f32) * conv).astype(bf16)
    gk_ref[...] = (dkv * value_ref[...].astype(f32)).astype(bf16)
    gv_ref[...] = (dkv * key_ref[...].astype(f32)).astype(bf16)


def call(kernel, out, *args, scratch=(), flops=0, any_space=0, name=None):
    nbytes = sum(math.prod(a.shape) * a.dtype.itemsize for a in args)
    vmem = pl.BlockSpec(memory_space=pltpu.VMEM)
    return pl.pallas_call(
        kernel,
        out_shape=out,
        in_specs=[vmem] * (len(args) - any_space)
        + [pl.BlockSpec(memory_space=pl.ANY)] * any_space,
        out_specs=jax.tree.map(lambda _: vmem, out),
        scratch_shapes=[pltpu.VMEM(shape, f32) for shape in scratch],
        compiler_params=pltpu.CompilerParams(vmem_limit_bytes=40 * 2**20),
        cost_estimate=pl.CostEstimate(flops=flops, bytes_accessed=nbytes, transcendentals=0),
        name=name,
    )(*args)


def local(query_gate, key_gate, value_gate, grad_out, long_filter):
    chans, seq = long_filter.shape
    half = seq // BLOCK
    groups = lax.axis_size("dp")
    total = query_gate.shape[1]
    both = 2 * chans
    tables = {name: jnp.asarray(table) for name, table in make_tables(half, seq).items()}
    forward, back = tables["forward"], tables["back"]
    turn, middle, lag_back = tables["turn"], tables["middle"], tables["lag"]
    query, key, value, grad = (
        x.reshape(total, BLOCK) for x in (query_gate, key_gate, value_gate, grad_out)
    )
    shape = jax.ShapeDtypeStruct
    pieces = shape((half, both, BLOCK), bf16)
    work = 2 * chans * half * 256 * 768

    gated = pl.pallas_call(
        gate_kernel,
        out_shape=pieces,
        in_specs=[pl.BlockSpec(memory_space=pltpu.HBM)] * 4,
        out_specs=pl.BlockSpec(memory_space=pltpu.VMEM),
        scratch_shapes=[
            pltpu.VMEM((4, total, BLOCK), bf16),
            pltpu.SemaphoreType.DMA((4, 4)),
        ],
        compiler_params=pltpu.CompilerParams(vmem_limit_bytes=63 * 2**20),
        cost_estimate=pl.CostEstimate(
            flops=total * BLOCK * 2, bytes_accessed=total * BLOCK * 12, transcendentals=0
        ),
        name="gate",
    )(key, value, grad, query)
    here = lax.all_to_all(
        gated, "ctx", 0, 0, tiled=True, axis_index_groups=[slots(half, FAR_IN)]
    )
    filter_spec = call(
        filter_kernel,
        shape((chans * half, 2 * BLOCK), f32),
        long_filter,
        forward,
        turn,
        middle,
        scratch=[(half * chans, BLOCK)],
        flops=2 * work,
        name="filter",
    )
    own = half // groups
    quads = groups // 2
    quad = (own, chans, BLOCK)
    vmem = pl.BlockSpec(memory_space=pltpu.VMEM)
    carried, keep, send = pl.pallas_call(
        transform_kernel,
        out_shape=(pieces, shape((2, 2, *quad), f32), shape((2, 2, *quad), bf16)),
        in_specs=[vmem] * 7,
        out_specs=(pl.BlockSpec(memory_space=pltpu.HBM), vmem, vmem),
        scratch_shapes=[
            pltpu.VMEM((both * half, 2 * BLOCK), f32),
            pltpu.VMEM((half * both, BLOCK), f32),
            pltpu.VMEM((half * chans, BLOCK), f32),
            pltpu.VMEM((half, both, BLOCK), bf16),
            pltpu.SemaphoreType.DMA((2,)),
        ],
        compiler_params=pltpu.CompilerParams(vmem_limit_bytes=40 * 2**20),
        cost_estimate=pl.CostEstimate(flops=6 * work, bytes_accessed=2**21, transcendentals=0),
        name="transform",
    )(here, filter_spec, tables["exact"], back, lag_back, turn, middle)
    other = lax.ppermute(send, "dp", [(i, i ^ 2) for i in range(groups)])
    keep, send = call(
        core_kernel,
        (shape((2, *quad), f32), shape((2, *quad), bf16)),
        keep,
        other,
        flops=HINT,
        name="core",
    )
    cores = [[2 * z, 2 * z + 1] for z in range(quads)]
    other = lax.all_gather(send, "dp", axis=0, axis_index_groups=cores)
    keep, send = call(
        halve_kernel,
        (shape(quad, f32), shape(quad, bf16)),
        keep,
        other,
        name="halve",
    )
    sides = [[i, i + 4] for i in range(groups // 2)]
    other = lax.all_gather(send, "dp", axis=0, axis_index_groups=sides)
    back_here = lax.all_to_all(
        carried, "ctx", 0, 0, tiled=True, axis_index_groups=[slots(half, FAR_OUT)]
    )
    *grads, grad_filter = call(
        functools.partial(final_kernel, scale=1.0 / math.sqrt(seq * groups)),
        (shape((total, BLOCK), bf16),) * 3 + (shape((chans, own * BLOCK), f32),),
        back_here,
        key,
        value,
        grad,
        keep,
        other,
        name="final",
    )
    return tuple(g[None] for g in grads) + (grad_filter,)


def solution(mesh):
    in_specs = (
        P("dp", None, "ctx"),
        P("dp", None, "ctx"),
        P("dp", None, "ctx"),
        P("dp", None, "ctx"),
        P("ctx", None),
    )
    out_specs = (P("dp", None, "ctx"), P("dp", None, "ctx"), P("dp", None, "ctx"), P("ctx", "dp"))
    return jax.shard_map(local, mesh=mesh, in_specs=in_specs, out_specs=out_specs, check_vma=False)
```
